32 devices in a mesh: section: 2 (over x), dp: 4 (over z), mp: 4 (over y, core).
Axes of the slice: x: 2, y: 2, z: 4, core: 2. Of those that a mesh axis runs over, the one named last changes fastest.
Arguments:
- inputs: bfloat16 [2, 8, 128, 4096], P('section', 'dp'), may hold values from -6 to 6
- norm_gains: bfloat16 [2, 4096], P('section'), may hold values from 0.5 to 1.5
- weights: bfloat16 [2, 4096, 4, 4096], P('section', 'dp', None, 'mp'), may hold values from -0.09375 to 0.09375
- cotangent: bfloat16 [8, 128, 4096], P('dp'), may hold values from -6 to 6
- lengths: int32 [2, 8], P(None, 'dp'), may hold values from 32 to 128, as said below
- dp_noise: float32 [2, 4096, 4, 4096], P('section', 'dp', None, 'mp'), may hold values from -6 to 6
Outputs:
- noisy_grad: float32 [2, 4096, 4, 4096], P('section', 'dp', None, 'mp')
- clip_scale: float32 [8], P('dp')
The draws below stay inside these ranges and needn't reach their ends.
Inputs may be any that keep to these rules, and one draw needn't show every extreme that they name: `lengths`: the first example of each row has length 128.
All inputs are finite; a program needn't handle non-finite values.
Results may differ from the reference program's by a relative error of at most 0.024.
Values may be sent and summed in bfloat16 or wider, within the bound.
No kernel may reach another device: no remote copies, remote signals or barrier semaphores. Data moves between devices by JAX's collectives and lax.ppermute only.
A program may use at most 320 MiB of HBM per device.

```python
import jax
import jax.numpy as jnp
from jax import lax

D = 4096
HEAD = 64
S = 128
MB = 2
INNER = 4096
EXAMPLES = 8
N_DP = 4
N_MP = 4


def draw_lengths(key, part):
    drawn = jax.random.randint(key, (2, EXAMPLES), S // 4, S + 1, dtype=jnp.int32)
    column = jnp.arange(EXAMPLES)[None, :]
    return jnp.where(column == 0, S, drawn).astype(jnp.int32)


def block_scale(rng, dims, split, least, largest):
    gain = 1.0
    for dim, parts in split:
        heights = jax.random.uniform(jax.random.fold_in(jax.random.fold_in(rng, 6), dim), (parts,), jnp.float32, least / len(split), largest / len(split))
        gain = gain * jnp.repeat(jnp.exp(heights), dims[dim] // parts).reshape((-1,) + (1,) * (len(dims) - 1 - dim))
    return gain


def noise(rng, extent, spread, most, cuts=(), kind=jnp.bfloat16):
    values = spread * jax.random.normal(rng, extent, jnp.float32)
    if cuts:
        values = values * block_scale(rng, extent, cuts, -0.22, 0.18)
    return jnp.clip(values, -most, most).astype(kind)


def setup_inputs(seed: int = 0) -> dict:
    streams_of = jax.random.split(jax.random.key(seed), 7)
    return {
        "inputs": noise(streams_of[0], (2, EXAMPLES, S, D), 1.0, 6.0, ((0, 2), (1, 4))),
        "norm_gains": jnp.clip(1.0 + 0.1 * jax.random.normal(streams_of[1], (2, D), jnp.float32), 0.5, 1.5).astype(jnp.bfloat16),
        "weights": noise(streams_of[2], (2, D, 4, INNER), D ** -0.5, 0.09375, ((0, 2), (1, 4), (3, 4))),
        "cotangent": noise(streams_of[3], (EXAMPLES, S, D), 1.0, 6.0, ((0, 4),)),
        "lengths": draw_lengths(jax.random.fold_in(streams_of[6], 71), 0),
        "dp_noise": noise(streams_of[5], (2, D, 4, INNER), 1.0, 6.0, ((0, 2), (1, 4), (3, 4)), jnp.float32),
    }


def rms_norm(values_in, gain_row):
    value32 = values_in.astype(jnp.float32)
    inverse = lax.rsqrt(lax.optimization_barrier(jnp.mean(value32 * value32, axis=-1, keepdims=True)) + 1e-06)
    return (value32 * inverse * gain_row.astype(jnp.float32)).astype(jnp.bfloat16)

def project(left, right):
    return jnp.dot(left, right, preferred_element_type=jnp.float32).astype(jnp.bfloat16)

def attend(queries, key_proj, value_proj, key_mask):
    seq_len = queries.shape[0]
    query_heads = queries.reshape(seq_len, -1, HEAD).astype(jnp.float32)
    key_heads = key_proj.reshape(seq_len, -1, HEAD).astype(jnp.float32)
    value_heads = value_proj.reshape(seq_len, -1, HEAD).astype(jnp.float32)
    scores = jnp.einsum('shd,thd->hst', query_heads, key_heads) * HEAD ** (-0.5)
    scores = jnp.where(key_mask[None, None, :], scores, -jnp.inf)
    attn_probs = jax.nn.softmax(scores, axis=-1)
    probs_low = attn_probs.astype(jnp.bfloat16).astype(jnp.float32)
    context = jnp.einsum('hst,thd->shd', probs_low, value_heads).reshape(seq_len, -1)
    return (attn_probs, context.astype(jnp.bfloat16))

def attend_back(queries, key_proj, value_proj, attn_probs, grad_ctx):
    seq_len = queries.shape[0]
    query_heads = queries.reshape(seq_len, -1, HEAD).astype(jnp.float32)
    key_heads = key_proj.reshape(seq_len, -1, HEAD).astype(jnp.float32)
    value_heads = value_proj.reshape(seq_len, -1, HEAD).astype(jnp.float32)
    grad_heads = grad_ctx.reshape(seq_len, -1, HEAD).astype(jnp.float32)
    grad_probs = jnp.einsum('shd,thd->hst', grad_heads, value_heads)
    inner_sum = lax.optimization_barrier(jnp.sum(grad_probs * attn_probs, axis=-1, keepdims=True))
    grad_scores = (attn_probs * (grad_probs - inner_sum) * HEAD ** (-0.5)).astype(jnp.bfloat16).astype(jnp.float32)
    probs_low = attn_probs.astype(jnp.bfloat16).astype(jnp.float32)
    grad_query = jnp.einsum('hst,thd->shd', grad_scores, key_heads).reshape(seq_len, -1)
    grad_key = jnp.einsum('hst,shd->thd', grad_scores, query_heads).reshape(seq_len, -1)
    grad_value = jnp.einsum('hst,shd->thd', probs_low, grad_heads).reshape(seq_len, -1)
    return (grad_query.astype(jnp.bfloat16), grad_key.astype(jnp.bfloat16), grad_value.astype(jnp.bfloat16))

def group_terms(left, right):
    seq_len = left.shape[0]
    left_groups = left.reshape(seq_len, N_MP, -1).astype(jnp.float32)
    right_groups = right.reshape(right.shape[0], N_MP, -1).astype(jnp.float32)
    return jnp.einsum('srj,drj->rsd', left_groups, right_groups)

def group_sum(terms):
    return lax.optimization_barrier(jnp.sum(terms.astype(jnp.bfloat16).astype(jnp.float32), axis=0))

def gram(matrix):
    return jnp.dot(matrix, matrix.T, preferred_element_type=jnp.float32)

def ghost(normed, kv_rows, grad_query, grad_key, grad_value, grad_out, context):
    first = jnp.sum(gram(normed) * gram(grad_query))
    second = jnp.sum(gram(kv_rows) * (gram(grad_key) + gram(grad_value)))
    third = jnp.sum(gram(grad_out) * gram(context))
    return first + second + third

def one_example(enc_in, dec_in, cot_rows, enc_len, dec_len, norm_gains, weights):
    positions = jnp.arange(S)
    key_mask = positions < enc_len
    enc_w = weights[0]
    dec_w = weights[1]
    normed_enc = rms_norm(enc_in, norm_gains[0])
    query_enc = project(normed_enc, enc_w[:, 0])
    key_enc = project(normed_enc, enc_w[:, 1])
    value_enc = project(normed_enc, enc_w[:, 2])
    probs_enc, context_enc = attend(query_enc, key_enc, value_enc, key_mask)
    enc_out = (enc_in.astype(jnp.float32) + group_sum(group_terms(context_enc, enc_w[:, 3]))).astype(jnp.bfloat16)
    normed_dec = rms_norm(dec_in, norm_gains[1])
    query_dec = project(normed_dec, dec_w[:, 0])
    key_dec = project(enc_out, dec_w[:, 1])
    value_dec = project(enc_out, dec_w[:, 2])
    probs_dec, context_dec = attend(query_dec, key_dec, value_dec, key_mask)
    grad_out_dec = cot_rows * (positions < dec_len).astype(jnp.bfloat16)[:, None]
    grad_ctx_dec = project(grad_out_dec, dec_w[:, 3])
    gq_dec, gk_dec, gv_dec = attend_back(query_dec, key_dec, value_dec, probs_dec, grad_ctx_dec)
    grad_enc = group_sum(group_terms(gk_dec, dec_w[:, 1]) + group_terms(gv_dec, dec_w[:, 2])).astype(jnp.bfloat16)
    grad_ctx_enc = project(grad_enc, enc_w[:, 3])
    gq_enc, gk_enc, gv_enc = attend_back(query_enc, key_enc, value_enc, probs_enc, grad_ctx_enc)
    sq_norm = ghost(normed_enc, normed_enc, gq_enc, gk_enc, gv_enc, grad_enc, context_enc)
    sq_norm = sq_norm + ghost(normed_dec, enc_out, gq_dec, gk_dec, gv_dec, grad_out_dec, context_dec)
    enc_pairs = (normed_enc, gq_enc, normed_enc, gk_enc, normed_enc, gv_enc, grad_enc, context_enc)
    dec_pairs = (normed_dec, gq_dec, enc_out, gk_dec, enc_out, gv_dec, grad_out_dec, context_dec)
    return (sq_norm, enc_pairs, dec_pairs)

def weighted_sum(left_all, right_all, clip_scale):
    left_groups = left_all.reshape(N_DP, MB, S, left_all.shape[-1])
    right_groups = right_all.reshape(N_DP, MB, S, right_all.shape[-1])
    scale_groups = clip_scale.reshape(N_DP, MB)

    def add_group(carry, items):
        left_block, right_block, scale_block = items
        partial_value = jnp.einsum('i,isd,isj->dj', scale_block, left_block.astype(jnp.float32), right_block.astype(jnp.float32))
        return (carry + partial_value.astype(jnp.bfloat16).astype(jnp.float32), None)
    start_sum = jnp.zeros((left_all.shape[-1], right_all.shape[-1]), jnp.float32)
    result, unused = lax.scan(add_group, start_sum, (left_groups, right_groups, scale_groups))
    return result

def reference(inputs, norm_gains, weights, cotangent, lengths, dp_noise):
    run = jax.vmap(one_example, in_axes=(0, 0, 0, 0, 0, None, None))
    sq_norm, enc_pairs, dec_pairs = run(inputs[0], inputs[1], cotangent, lengths[0], lengths[1], norm_gains, weights)
    bound = jnp.sqrt(jnp.float32(8.0 * D * INNER))
    clip_scale = bound / (jnp.sqrt(sq_norm) + 0.01 * bound)
    layers = []
    for pairs in (enc_pairs, dec_pairs):
        mats = [weighted_sum(pairs[2 * slot], pairs[2 * slot + 1], clip_scale) for slot in range(4)]
        layers.append(jnp.stack(mats, axis=1))
    summed = jnp.stack(layers, axis=0)
    noisy_grad = (summed + dp_noise) / EXAMPLES
    return (noisy_grad, clip_scale)
```

```python
import functools

import jax
import jax.numpy as jnp
from jax import lax
from jax.experimental import pallas as pl
from jax.experimental.pallas import tpu as pltpu
from jax.sharding import PartitionSpec as P

D = 4096
HEADS = 64
HEAD = 64
PAIR = 2 * HEAD
F32 = jnp.float32
BF16 = jnp.bfloat16
NN = (((1,), (0,)), ((), ()))
NT = (((1,), (1,)), ((), ()))
TN = (((0,), (0,)), ((), ()))


def mm(left, right, dims=NN):
    return lax.dot_general(left, right, dims, preferred_element_type=F32)


def dp_shift(x, distance, sections):
    n = lax.axis_size("dp")
    pairs = [(s * n + i, s * n + (i ^ distance)) for s in sections for i in range(n)]
    return lax.ppermute(x, ("section", "dp"), pairs)


def mp_shift(x, distance, sections, flip=False):
    n = lax.axis_size("mp")
    pairs = [
        (s * n + i, (1 - s if flip else s) * n + (i ^ distance)) for s in sections for i in range(n)
    ]
    return lax.ppermute(x, ("section", "mp"), pairs)


def pick(parts, index):
    return lax.dynamic_index_in_dim(parts, index, 0, keepdims=False)


def to_owner(parts, sections):
    n = lax.axis_size("dp")
    me = lax.axis_index("dp")
    got = [dp_shift(pick(parts, me ^ s), s, sections) for s in range(n - 1, 0, -1)]
    return [pick(parts, me)] + got


def in_order(slots):
    me = lax.axis_index("dp")
    stacked = jnp.stack(slots)
    return jnp.stack([pick(stacked, me ^ i) for i in range(len(slots))])


def gather(rows, sections):
    n = lax.axis_size("dp")
    got = {s: dp_shift(rows, s, sections) for s in range(n - 1, 0, -1)}
    return in_order([rows] + [got[s] for s in range(1, n)])


def halves(mine, other, parity):
    return jnp.where(
        parity == 0,
        jnp.concatenate([mine, other], axis=-2),
        jnp.concatenate([other, mine], axis=-2),
    )


def to_columns(rows, parity, sections):
    n = lax.axis_size("dp")
    me = lax.axis_index("dp")
    k, seq, full = rows.shape
    half, width = seq // 2, full // n
    mine = [
        lax.dynamic_slice(rows, (0, parity * half, (me ^ s) * width), (k, half, width))
        for s in range(n)
    ]
    got = {s: dp_shift(mine[s], s, sections) for s in range(n - 1, 0, -1)}
    return in_order([mine[0]] + [got[s] for s in range(1, n)])


def relay(terms, residual, source):
    groups = lax.axis_size("mp") // 2
    index = lax.axis_index("mp")
    parity = index % 2
    half = terms.shape[1] // 2
    low = terms.astype(BF16)
    keep = lax.dynamic_slice_in_dim(low, parity * half, half, 1)
    give = lax.dynamic_slice_in_dim(low, (1 - parity) * half, half, 1)
    total = keep.astype(F32) + mp_shift(give, 1, (source,)).astype(F32)
    if residual is not None:
        total = total + jnp.where(index < 2, residual.astype(F32), 0.0)
    total = total.astype(BF16)
    got = [mp_shift(total, 2 * g, (source,), flip=True).astype(F32) for g in range(groups)]
    mine = functools.reduce(jnp.add, got).astype(BF16)
    other = mp_shift(mine, 1, (1 - source,))
    return halves(mine, other, parity)


def add_up(sources, start):
    terms = [ref[:, offset + start : offset + start + PAIR] for ref, offset in sources]
    if len(terms) == 1:
        return terms[0]
    return functools.reduce(jnp.add, [t.astype(F32) for t in terms]).astype(BF16)


def pair_masks(seq):
    lane = lax.broadcasted_iota(jnp.int32, (seq, PAIR), 1)
    return lane < HEAD


def stack_heads(x, first):
    zero = jnp.zeros_like(x)
    return jnp.concatenate([jnp.where(first, x, zero), jnp.where(first, zero, x)], axis=0)


def softmax_pair(scores, valid):
    seq = scores.shape[0]
    out = []
    for h in range(2):
        s = jnp.where(valid, scores[:, h * seq : (h + 1) * seq] * HEAD**-0.5, -jnp.inf)
        e = jnp.exp(s - jnp.max(s, axis=1, keepdims=True))
        out.append(e / jnp.sum(e, axis=1, keepdims=True))
    return jnp.concatenate(out, axis=1)


def bind(plan, refs):
    return [[(refs[i], offset) for i, offset in sources] for sources in plan]


def fwd_kernel(plan, count, info, *refs):
    qs, ks, vs = bind(plan, refs)
    ctx_ref = refs[count]
    seq, width = ctx_ref.shape

    @pl.when(info[0] == 1)
    def run():
        first = pair_masks(seq)
        valid = lax.broadcasted_iota(jnp.int32, (seq, seq), 1) < info[1]
        for c in range(0, width, PAIR):
            q, k, v = add_up(qs, c), add_up(ks, c), add_up(vs, c)
            probs = softmax_pair(mm(q, stack_heads(k, first), NT), valid)
            ctx = mm(probs.astype(BF16), stack_heads(v, first))
            ctx_ref[:, c : c + PAIR] = ctx.astype(BF16)


def full_kernel(plan, count, decoder, info, *refs):
    qs, ks, vs, gs = bind(plan, refs)
    kv_ref, send_ref, gram_ref = refs[count:]
    seq = kv_ref.shape[0]
    width = kv_ref.shape[1] // 2

    @pl.when(info[0] == 1)
    def run():
        first = pair_masks(seq)
        valid = lax.broadcasted_iota(jnp.int32, (seq, seq), 1) < info[1]
        grams = [jnp.zeros((seq, seq), F32) for _ in range(3)]
        for c in range(0, width, PAIR):
            q, k, v, g = add_up(qs, c), add_up(ks, c), add_up(vs, c), add_up(gs, c)
            k2, v2 = stack_heads(k, first), stack_heads(v, first)
            probs = softmax_pair(mm(q, k2, NT), valid)
            low = probs.astype(BF16)
            ctx = mm(low, v2).astype(BF16)
            gp = mm(g, v2, NT)
            ds = []
            for h in range(2):
                part = slice(h * seq, (h + 1) * seq)
                p, gph = probs[:, part], gp[:, part]
                inner = jnp.sum(gph * p, axis=1, keepdims=True)
                ds.append((p * (gph - inner) * HEAD**-0.5).astype(BF16))
            ds = jnp.concatenate(ds, axis=1)
            gq = mm(ds, k2).astype(BF16)
            gk = mm(ds, q, TN)
            gk = jnp.where(first, gk[:seq], gk[seq:]).astype(BF16)
            gv = mm(low, g, TN)
            gv = jnp.where(first, gv[:seq], gv[seq:]).astype(BF16)
            kv_ref[:, c : c + PAIR] = gk
            kv_ref[:, width + c : width + c + PAIR] = gv
            send_ref[:, c : c + PAIR] = gq
            send_ref[:, width + c : width + c + PAIR] = ctx if decoder else gk
            send_ref[:, 2 * width + c : 2 * width + c + PAIR] = gv
            grams[0] += mm(gq, gq, NT)
            grams[1] += mm(gk, gk, NT) + mm(gv, gv, NT)
            grams[2] += mm(ctx, ctx, NT)
        for i in range(3):
            gram_ref[i] = grams[i]


def call_attention(kernel, info, operands, outs, flops, name):
    arrays, plan = [], []
    for sources in operands:
        plan.append([])
        for array, offset in sources:
            known = [i for i, a in enumerate(arrays) if a is array]
            if not known:
                arrays.append(array)
            plan[-1].append((known[0] if known else len(arrays) - 1, offset))
    vmem = pl.BlockSpec(memory_space=pltpu.VMEM)
    return pl.pallas_call(
        functools.partial(kernel, plan, len(arrays)),
        out_shape=outs,
        in_specs=[pl.BlockSpec(memory_space=pltpu.SMEM)] + [vmem] * len(arrays),
        out_specs=(vmem,) * len(outs),
        compiler_params=pltpu.CompilerParams(vmem_limit_bytes=32 << 20),
        cost_estimate=pl.CostEstimate(
            flops=flops, bytes_accessed=sum(2 * a.size for a in arrays), transcendentals=0
        ),
        name=name,
    )(info, *arrays)


def attend(info, operands, seq, width):
    rows = jax.ShapeDtypeStruct((seq, width), BF16)
    return call_attention(fwd_kernel, info, operands, (rows,), 8 * seq * seq * width, "attend")[0]


def attend_back(info, operands, seq, width, decoder):
    outs = (
        jax.ShapeDtypeStruct((seq, 2 * width), BF16),
        jax.ShapeDtypeStruct((seq, 3 * width), BF16),
        jax.ShapeDtypeStruct((3, seq, seq), F32),
    )

    def kernel(plan, count, *refs):
        full_kernel(plan, count, decoder, *refs)

    return call_attention(kernel, info, operands, outs, 40 * seq * seq * width, "attend_back")


def wgrad_kernel(mb, chunk, scale, clip, info, *refs):
    x1, xa, xb = refs[:mb], refs[mb : 2 * mb], refs[2 * mb : 3 * mb]
    send, swap = refs[3 * mb : 4 * mb], refs[4 * mb : 5 * mb]
    noise, out = refs[5 * mb :]
    width = out.shape[2]
    count = x1[0].shape[0] // chunk
    is_dec = info[0] == 1

    def clipped(group):
        return [
            jnp.concatenate(
                [
                    (ref[i * chunk : (i + 1) * chunk].astype(F32) * clip[b * count + i]).astype(BF16)
                    for i in range(count)
                ],
                axis=0,
            )
            for b, ref in enumerate(group)
        ]

    def put(slot, lefts, rights, first):
        total = functools.reduce(
            jnp.add, [mm(x, y[:, first : first + width], TN) for x, y in zip(lefts, rights)]
        )
        out[:, slot, :] = (total + noise[:, slot, :]) * scale

    l1, la, lb = clipped(x1), clipped(xa), clipped(xb)
    put(0, l1, send, 0)

    @pl.when(is_dec)
    def decoder():
        put(1, lb, swap, 0)
        put(2, lb, send, 2 * width)
        put(3, la, send, width)

    @pl.when(jnp.logical_not(is_dec))
    def encoder():
        put(1, la, send, width)
        put(2, l1, send, 2 * width)
        put(3, lb, swap, 0)


def wgrad(clip, info, x1, xa, xb, send, swap, noise, chunk, examples):
    mb = len(x1)
    tokens, depth = x1[0].shape
    width = noise.shape[2]
    block = 128
    smem = pl.BlockSpec(memory_space=pltpu.SMEM)
    left = pl.BlockSpec((tokens, block), lambda i: (0, i))
    wide = pl.BlockSpec((block, 4, width), lambda i: (i, 0, 0))
    once = [
        pl.BlockSpec(y.shape, lambda i: (0, 0), pipeline_mode=pl.Buffered(1)) for y in send + swap
    ]
    return pl.pallas_call(
        functools.partial(wgrad_kernel, mb, chunk, 1.0 / examples),
        grid=(depth // block,),
        out_shape=jax.ShapeDtypeStruct(noise.shape, F32),
        in_specs=[smem, smem] + [left] * (3 * mb) + once + [wide],
        out_specs=wide,
        compiler_params=pltpu.CompilerParams(vmem_limit_bytes=56 << 20),
        cost_estimate=pl.CostEstimate(
            flops=8 * mb * tokens * depth * width,
            bytes_accessed=depth * 4 * width * 8 + mb * tokens * width * 8,
            transcendentals=0,
        ),
        name="weight_gradient",
    )(clip, info, *x1, *xa, *xb, *send, *swap, noise)


def per_device(inputs, norm_gains, weights, cotangent, lengths, dp_noise):
    section = lax.axis_index("section")
    is_dec = section == 1
    me = lax.axis_index("dp")
    parity = lax.axis_index("mp") % 2
    n = lax.axis_size("dp")
    mb = inputs.shape[1]
    seq = inputs.shape[2]
    depth = weights.shape[1]
    inner = weights.shape[3]
    both, enc, dec = (0, 1), (0,), (1,)
    w = lax.optimization_barrier(jnp.transpose(weights[0], (1, 0, 2)))
    gain = norm_gains[0].astype(F32)
    gain_cols = lax.dynamic_slice_in_dim(gain, me * depth, depth)

    def rows_of(x):
        return x.reshape(n * seq, x.shape[-1])

    def owner_gram(x, sections):
        terms = jnp.einsum("bntd,bnud->nbtu", x, x, preferred_element_type=F32)
        return functools.reduce(jnp.add, to_owner(terms, sections))

    def info(flag, b):
        return jnp.stack([flag.astype(jnp.int32), lengths[0, b]])

    own32 = inputs[0].astype(F32)
    inv = lax.rsqrt(jnp.mean(own32 * own32, axis=-1) + 1e-06)
    inv_all = gather(inv, both)
    raw_half, x = [], []
    for b in range(mb):
        mine = to_columns(inputs[0, b : b + 1], parity, both)[:, 0]
        raw = halves(mine, mp_shift(mine, 1, both), parity)
        raw_half.append(mine)
        x.append(rows_of((raw.astype(F32) * inv_all[:, b, :, None] * gain_cols).astype(BF16)))
    keep = (jnp.arange(seq)[None] < lengths[1][:, None]).astype(BF16)
    cot = cotangent * keep[:, :, None]
    cot_half = to_columns(cot, parity, dec)
    cot_cols = halves(cot_half, mp_shift(cot_half, 1, dec), parity)
    cot_cols = [rows_of(cot_cols[:, b]) for b in range(mb)]
    first = []
    for b in range(mb):
        if b < mb - 1:
            parts = [mm(x[b], w[s]) for s in range(3)]
        else:
            w_k, w_v = jnp.where(is_dec, w[3], w[1]), jnp.where(is_dec, w[3], w[2])
            parts = [
                mm(x[b], w[0]),
                mm(jnp.where(is_dec, cot_cols[0], x[b]), w_k),
                mm(jnp.where(is_dec, cot_cols[1], x[b]), w_v),
            ]
        parts = jnp.concatenate([p.astype(BF16) for p in parts], axis=1)
        first.append(
            lax.psum_scatter(
                parts.reshape(n, seq, 3 * inner), "dp", scatter_dimension=0, tiled=False
            )
        )
    ctx_all, enc_out = [], []
    for b in range(mb):
        qkv = [[(first[b], i * inner)] for i in range(3)]
        ctx = attend(info(section == 0, b), qkv, seq, inner)
        ctx_all.append(rows_of(gather(ctx, enc)))
        terms = mm(ctx_all[b], w[3], NT).reshape(n, seq, depth)
        enc_out.append(relay(terms, raw_half[b], 0))
    gk_all, grad_enc, dec_send, dec_gram = [], [], [], []
    for b in range(mb):
        rows = rows_of(enc_out[b])
        parts = [mm(rows, w[s]).astype(BF16) for s in (1, 2)]
        kv = to_owner(jnp.concatenate(parts, axis=1).reshape(n, seq, 2 * inner), dec)
        operands = [
            [(first[b], 0)],
            [(part, 0) for part in kv],
            [(part, inner) for part in kv],
            [(first[mb - 1], (1 + b) * inner)],
        ]
        gkv, send, gram = attend_back(info(section == 1, b), operands, seq, inner, True)
        gkv_all = rows_of(gather(gkv, dec))
        terms = mm(gkv_all[:, :inner], w[1], NT) + mm(gkv_all[:, inner:], w[2], NT)
        grad_enc.append(relay(terms.reshape(n, seq, depth), None, 1))
        gk_all.append(gkv_all[:, :inner])
        dec_send.append(send)
        dec_gram.append(gram)
    gram_enc_out = owner_gram(jnp.stack(enc_out), dec)
    enc_send, enc_gram = [], []
    for b in range(mb):
        gctx = to_owner(mm(rows_of(grad_enc[b]), w[3]).astype(BF16).reshape(n, seq, inner), enc)
        operands = [[(first[b], i * inner)] for i in range(3)] + [[(part, 0) for part in gctx]]
        unused, send, gram = attend_back(info(section == 0, b), operands, seq, inner, False)
        enc_send.append(send)
        enc_gram.append(gram)
    gram_grad_enc = owner_gram(jnp.stack(grad_enc), enc)
    send_all = [
        lax.all_gather(jnp.where(is_dec, d, e), "dp", axis=0, tiled=True)
        for d, e in zip(dec_send, enc_send)
    ]
    normed = (own32 * inv[..., None] * gain).astype(BF16)
    gram_x = jnp.einsum("btd,bud->btu", normed, normed, preferred_element_type=F32)
    gram_cot = jnp.einsum("btd,bud->btu", cot, cot, preferred_element_type=F32)
    dg, eg = jnp.stack(dec_gram, axis=1), jnp.stack(enc_gram, axis=1)
    dec_sq = jnp.sum(gram_x * dg[0] + gram_enc_out * dg[1] + gram_cot * dg[2], axis=(1, 2))
    enc_sq = jnp.sum(gram_x * (eg[0] + eg[1]) + gram_grad_enc * eg[2], axis=(1, 2))
    sq = jnp.where(is_dec, dec_sq, enc_sq)
    step = 1
    while step < lax.axis_size("mp"):
        sq = sq + mp_shift(sq, step, both)
        step *= 2
    sq = sq + mp_shift(sq, 0, both, flip=True)
    bound = jnp.sqrt(jnp.float32(8.0 * D * HEADS * HEAD))
    clip = bound / (jnp.sqrt(sq) + 0.01 * bound)
    clip_all = gather(clip, both).T.reshape(-1)
    xa = [jnp.where(is_dec, c, r) for c, r in zip(cot_cols, x)]
    xb = [rows_of(jnp.where(is_dec, o, g)) for o, g in zip(enc_out, grad_enc)]
    swap = [jnp.where(is_dec, k, c) for k, c in zip(gk_all, ctx_all)]
    flag = section.astype(jnp.int32)[None]
    out = wgrad(clip_all, flag, x, xa, xb, send_all, swap, dp_noise[0], seq, mb * n)
    return (out[None], clip)


def solution(mesh):
    placed = (
        P("section", "dp", None, None),
        P("section", None),
        P("section", "dp", None, "mp"),
        P("dp", None, None),
        P(None, "dp"),
        P("section", "dp", None, "mp"),
    )
    return jax.shard_map(
        per_device,
        mesh=mesh,
        in_specs=placed,
        out_specs=(P("section", "dp", None, "mp"), P("dp")),
        check_vma=False,
    )
```

```python
import functools

import jax
import jax.numpy as jnp
from jax import lax
from jax.experimental import pallas as pl
from jax.experimental.pallas import tpu as pltpu
from jax.sharding import PartitionSpec as P

D = 4096
HEADS = 64
HEAD = 64
PAIR = 2 * HEAD
F32 = jnp.float32
BF16 = jnp.bfloat16
NN = (((1,), (0,)), ((), ()))
NT = (((1,), (1,)), ((), ()))
TN = (((0,), (0,)), ((), ()))


def mm(left, right, dims=NN):
    return lax.dot_general(left, right, dims, preferred_element_type=F32)


def dp_shift(x, distance, sections):
    n = lax.axis_size("dp")
    pairs = [(s * n + i, s * n + (i ^ distance)) for s in sections for i in range(n)]
    return lax.ppermute(x, ("section", "dp"), pairs)


def mp_shift(x, distance, sections, flip=False):
    n = lax.axis_size("mp")
    pairs = [
        (s * n + i, (1 - s if flip else s) * n + (i ^ distance)) for s in sections for i in range(n)
    ]
    return lax.ppermute(x, ("section", "mp"), pairs)


def pick(parts, index):
    return lax.dynamic_index_in_dim(parts, index, 0, keepdims=False)


def to_owner(parts, sections):
    n = lax.axis_size("dp")
    me = lax.axis_index("dp")
    got = [dp_shift(pick(parts, me ^ s), s, sections) for s in range(n - 1, 0, -1)]
    return [pick(parts, me)] + got


def in_order(slots):
    me = lax.axis_index("dp")
    stacked = jnp.stack(slots)
    return jnp.stack([pick(stacked, me ^ i) for i in range(len(slots))])


def gather(rows, sections):
    n = lax.axis_size("dp")
    got = {s: dp_shift(rows, s, sections) for s in range(n - 1, 0, -1)}
    return in_order([rows] + [got[s] for s in range(1, n)])


def halves(mine, other, parity):
    return jnp.where(
        parity == 0,
        jnp.concatenate([mine, other], axis=-2),
        jnp.concatenate([other, mine], axis=-2),
    )


def to_columns(rows, parity, sections):
    n = lax.axis_size("dp")
    me = lax.axis_index("dp")
    k, seq, full = rows.shape
    half, width = seq // 2, full // n
    mine = [
        lax.dynamic_slice(rows, (0, parity * half, (me ^ s) * width), (k, half, width))
        for s in range(n)
    ]
    got = {s: dp_shift(mine[s], s, sections) for s in range(n - 1, 0, -1)}
    return in_order([mine[0]] + [got[s] for s in range(1, n)])


def relay(terms, residual, sources, giver, targets):
    groups = lax.axis_size("mp") // 2
    index = lax.axis_index("mp")
    parity = index % 2
    half = terms.shape[1] // 2
    low = terms.astype(BF16)
    keep = lax.dynamic_slice_in_dim(low, parity * half, half, 1)
    give = lax.dynamic_slice_in_dim(low, (1 - parity) * half, half, 1)
    total = keep.astype(F32) + mp_shift(give, 1, sources).astype(F32)
    if residual is not None:
        total = total + jnp.where(index < 2, residual.astype(F32), 0.0)
    total = total.astype(BF16)
    got = [mp_shift(total, 2 * g, (giver,), flip=True) for g in range(groups - 1, -1, -1)]
    got += [mp_shift(total, 2 * g, (0,)) for g in range(1, groups)]
    own = jnp.where(lax.axis_index("section") == 0, total.astype(F32), 0.0)
    mine = functools.reduce(jnp.add, [g.astype(F32) for g in got], own).astype(BF16)
    other = mp_shift(mine, 1, targets)
    return halves(mine, other, parity)


def add_up(sources, start):
    terms = [ref[:, offset + start : offset + start + PAIR] for ref, offset in sources]
    if len(terms) == 1:
        return terms[0]
    return functools.reduce(jnp.add, [t.astype(F32) for t in terms]).astype(BF16)


def pair_masks(seq):
    lane = lax.broadcasted_iota(jnp.int32, (seq, PAIR), 1)
    return lane < HEAD


def stack_heads(x, first):
    zero = jnp.zeros_like(x)
    return jnp.concatenate([jnp.where(first, x, zero), jnp.where(first, zero, x)], axis=0)


def softmax_pair(scores, valid):
    seq = scores.shape[0]
    out = []
    for h in range(2):
        s = jnp.where(valid, scores[:, h * seq : (h + 1) * seq] * HEAD**-0.5, -jnp.inf)
        e = jnp.exp(s - jnp.max(s, axis=1, keepdims=True))
        out.append(e / jnp.sum(e, axis=1, keepdims=True))
    return jnp.concatenate(out, axis=1)


def bind(plan, refs):
    return [[(refs[i], offset) for i, offset in sources] for sources in plan]


def fwd_kernel(plan, count, info, *refs):
    qs, ks, vs = bind(plan, refs)
    ctx_ref = refs[count]
    seq, width = ctx_ref.shape

    @pl.when(info[0] == 1)
    def run():
        first = pair_masks(seq)
        valid = lax.broadcasted_iota(jnp.int32, (seq, seq), 1) < info[1]
        for c in range(0, width, PAIR):
            q, k, v = add_up(qs, c), add_up(ks, c), add_up(vs, c)
            probs = softmax_pair(mm(q, stack_heads(k, first), NT), valid)
            ctx = mm(probs.astype(BF16), stack_heads(v, first))
            ctx_ref[:, c : c + PAIR] = ctx.astype(BF16)


def full_kernel(plan, count, decoder, info, *refs):
    qs, ks, vs, gs = bind(plan, refs)
    gk_ref, gv_ref, send_ref, gram_ref = refs[count:]
    seq, width = gk_ref.shape

    @pl.when(info[0] == 1)
    def run():
        first = pair_masks(seq)
        valid = lax.broadcasted_iota(jnp.int32, (seq, seq), 1) < info[1]
        grams = [jnp.zeros((seq, seq), F32) for _ in range(3)]
        for c in range(0, width, PAIR):
            q, k, v, g = add_up(qs, c), add_up(ks, c), add_up(vs, c), add_up(gs, c)
            k2, v2 = stack_heads(k, first), stack_heads(v, first)
            probs = softmax_pair(mm(q, k2, NT), valid)
            low = probs.astype(BF16)
            ctx = mm(low, v2).astype(BF16)
            gp = mm(g, v2, NT)
            ds = []
            for h in range(2):
                part = slice(h * seq, (h + 1) * seq)
                p, gph = probs[:, part], gp[:, part]
                inner = jnp.sum(gph * p, axis=1, keepdims=True)
                ds.append((p * (gph - inner) * HEAD**-0.5).astype(BF16))
            ds = jnp.concatenate(ds, axis=1)
            gq = mm(ds, k2).astype(BF16)
            gk = mm(ds, q, TN)
            gk = jnp.where(first, gk[:seq], gk[seq:]).astype(BF16)
            gv = mm(low, g, TN)
            gv = jnp.where(first, gv[:seq], gv[seq:]).astype(BF16)
            gk_ref[:, c : c + PAIR] = gk
            gv_ref[:, c : c + PAIR] = gv
            send_ref[:, c : c + PAIR] = gq
            send_ref[:, width + c : width + c + PAIR] = ctx if decoder else gk
            grams[0] += mm(gq, gq, NT)
            grams[1] += mm(gk, gk, NT) + mm(gv, gv, NT)
            grams[2] += mm(ctx, ctx, NT)
        for i in range(3):
            gram_ref[i] = grams[i]


def call_attention(kernel, info, operands, outs, flops, name, after=()):
    arrays, plan = [], []
    for sources in operands:
        plan.append([])
        for array, offset in sources:
            known = [i for i, a in enumerate(arrays) if a is array]
            if not known:
                arrays.append(array)
            plan[-1].append((known[0] if known else len(arrays) - 1, offset))
    vmem = pl.BlockSpec(memory_space=pltpu.VMEM)
    return pl.pallas_call(
        functools.partial(kernel, plan, len(arrays) + len(after)),
        out_shape=outs,
        in_specs=[pl.BlockSpec(memory_space=pltpu.SMEM)]
        + [vmem] * len(arrays)
        + [pl.BlockSpec(memory_space=pl.ANY)] * len(after),
        out_specs=(vmem,) * len(outs),
        compiler_params=pltpu.CompilerParams(vmem_limit_bytes=32 << 20),
        cost_estimate=pl.CostEstimate(
            flops=flops, bytes_accessed=sum(2 * a.size for a in arrays), transcendentals=0
        ),
        name=name,
    )(info, *arrays, *after)


def attend(info, operands, seq, width, after):
    rows = jax.ShapeDtypeStruct((seq, width), BF16)
    flops = 8 * seq * seq * width
    return call_attention(fwd_kernel, info, operands, (rows,), flops, "attend", after)[0]


def attend_back(info, operands, seq, width, decoder, after=()):
    outs = (
        jax.ShapeDtypeStruct((seq, width), BF16),
        jax.ShapeDtypeStruct((seq, width), BF16),
        jax.ShapeDtypeStruct((seq, 2 * width), BF16),
        jax.ShapeDtypeStruct((3, seq, seq), F32),
    )

    def kernel(plan, count, *refs):
        full_kernel(plan, count, decoder, *refs)

    flops = 40 * seq * seq * width
    return call_attention(kernel, info, operands, outs, flops, "attend_back", after)


def wgrad_kernel(mb, chunk, scale, clip, info, *refs):
    x1, xa, xb = refs[:mb], refs[mb : 2 * mb], refs[2 * mb : 3 * mb]
    send, kept, back = (refs[i * mb : (i + 1) * mb] for i in (3, 4, 5))
    noise, out = refs[6 * mb :]
    width = out.shape[2]
    count = x1[0].shape[0] // chunk
    is_dec = info[0] == 1

    def clipped(group):
        return [
            jnp.concatenate(
                [
                    (ref[i * chunk : (i + 1) * chunk].astype(F32) * clip[b * count + i]).astype(BF16)
                    for i in range(count)
                ],
                axis=0,
            )
            for b, ref in enumerate(group)
        ]

    def put(slot, lefts, rights, first):
        total = functools.reduce(
            jnp.add, [mm(x, y[:, first : first + width], TN) for x, y in zip(lefts, rights)]
        )
        out[:, slot, :] = (total + noise[:, slot, :]) * scale

    l1, la, lb = clipped(x1), clipped(xa), clipped(xb)
    put(0, l1, send, 0)

    @pl.when(is_dec)
    def decoder():
        put(1, lb, back, 0)
        put(2, lb, kept, 0)
        put(3, la, send, width)

    @pl.when(jnp.logical_not(is_dec))
    def encoder():
        put(1, la, send, width)
        put(2, l1, back, 0)
        put(3, lb, kept, 0)


def wgrad(clip, info, x1, xa, xb, send, kept, back, noise, chunk, examples):
    mb = len(x1)
    tokens, depth = x1[0].shape
    width = noise.shape[2]
    block = 256
    smem = pl.BlockSpec(memory_space=pltpu.SMEM)
    left = pl.BlockSpec((tokens, block), lambda i: (0, i))
    wide = pl.BlockSpec((block, 4, width), lambda i: (i, 0, 0))
    once = [
        pl.BlockSpec(y.shape, lambda i: (0, 0), pipeline_mode=pl.Buffered(1)) for y in send + kept + back
    ]
    return pl.pallas_call(
        functools.partial(wgrad_kernel, mb, chunk, 1.0 / examples),
        grid=(depth // block,),
        out_shape=jax.ShapeDtypeStruct(noise.shape, F32),
        in_specs=[smem, smem] + [left] * (3 * mb) + once + [wide],
        out_specs=wide,
        compiler_params=pltpu.CompilerParams(vmem_limit_bytes=56 << 20),
        cost_estimate=pl.CostEstimate(
            flops=8 * mb * tokens * depth * width,
            bytes_accessed=depth * 4 * width * 8 + mb * tokens * width * 8,
            transcendentals=0,
        ),
        name="weight_gradient",
    )(clip, info, *x1, *xa, *xb, *send, *kept, *back, noise)


def per_device(inputs, norm_gains, weights, cotangent, lengths, dp_noise):
    section = lax.axis_index("section")
    is_dec = section == 1
    me = lax.axis_index("dp")
    parity = lax.axis_index("mp") % 2
    n = lax.axis_size("dp")
    mb = inputs.shape[1]
    seq = inputs.shape[2]
    depth = weights.shape[1]
    inner = weights.shape[3]
    both, enc, dec = (0, 1), (0,), (1,)
    w = lax.optimization_barrier(jnp.transpose(weights[0], (1, 0, 2)))
    gain = norm_gains[0].astype(F32)
    gain_cols = lax.dynamic_slice_in_dim(gain, me * depth, depth)

    def rows_of(x):
        return x.reshape(n * seq, x.shape[-1])

    def owner_grams(x, sections):
        terms = jnp.einsum("bntd,bnud->nbtu", x, x, preferred_element_type=F32)
        return to_owner(terms, sections)

    def info(flag, b):
        return jnp.stack([flag.astype(jnp.int32), lengths[0, b]])

    own32 = inputs[0].astype(F32)
    inv = lax.rsqrt(jnp.mean(own32 * own32, axis=-1) + 1e-06)
    inv_all = gather(inv, both)
    raw_half, x = [], []
    for b in range(mb):
        mine = to_columns(inputs[0, b : b + 1], parity, both)[:, 0]
        raw = halves(mine, mp_shift(mine, 1, both), parity)
        raw_half.append(mine)
        x.append(rows_of((raw.astype(F32) * inv_all[:, b, :, None] * gain_cols).astype(BF16)))
    keep = (jnp.arange(seq)[None] < lengths[1][:, None]).astype(BF16)
    cot = cotangent * keep[:, :, None]
    cot_half = to_columns(cot, parity, dec)
    cot_cols = halves(cot_half, mp_shift(cot_half, 1, dec), parity)
    cot_cols = [rows_of(cot_cols[:, b]) for b in range(mb)]
    first = []
    for b in range(mb):
        if b < mb - 1:
            parts = [mm(x[b], w[s]) for s in range(3)]
        else:
            w_k, w_v = jnp.where(is_dec, w[3], w[1]), jnp.where(is_dec, w[3], w[2])
            parts = [
                mm(x[b], w[0]),
                mm(jnp.where(is_dec, cot_cols[0], x[b]), w_k),
                mm(jnp.where(is_dec, cot_cols[1], x[b]), w_v),
            ]
        parts = jnp.concatenate([p.astype(BF16) for p in parts], axis=1)
        first.append(
            lax.psum_scatter(
                parts.reshape(n, seq, 3 * inner), "dp", scatter_dimension=0, tiled=False
            )
        )
    w_relay = jnp.where(is_dec, w[2], mp_shift(w[1], 0, dec, flip=True))
    ctx_all, enc_out, kv_parts = [], [], []
    for b in range(mb):
        qkv = [[(first[b], i * inner)] for i in range(3)]
        after = [kv_parts[-1][1]] if b else []
        ctx = attend(info(section == 0, b), qkv, seq, inner, after)
        ctx_all.append(rows_of(gather(ctx, enc)))
        terms = mm(ctx_all[b], w[3], NT).reshape(n, seq, depth)
        enc_out.append(relay(terms, raw_half[b], enc, 0, both))
        terms = mm(rows_of(enc_out[b]), w_relay).astype(BF16).reshape(n, seq, inner)
        kv_parts.append(to_owner(terms, both))
    relay_all, grad_enc, dec_send, dec_gram = [], [], [], []
    for b in range(mb):
        parts = kv_parts[b]
        k = functools.reduce(jnp.add, [part.astype(F32) for part in parts]).astype(BF16)
        operands = [
            [(first[b], 0)],
            [(mp_shift(k, 0, enc, flip=True), 0)],
            [(part, 0) for part in parts],
            [(first[mb - 1], (1 + b) * inner)],
        ]
        gk, gv, send, gram = attend_back(info(section == 1, b), operands, seq, inner, True)
        rows = jnp.where(is_dec, gv, mp_shift(gk, 0, dec, flip=True))
        relay_all.append(rows_of(gather(rows, both)))
        terms = mm(relay_all[b], w_relay, NT).reshape(n, seq, depth)
        grad_enc.append(relay(terms, None, both, 1, enc))
        dec_send.append(send)
        dec_gram.append(gram)
    gram_enc_out = functools.reduce(jnp.add, owner_grams(jnp.stack(enc_out), dec))
    grad_grams = owner_grams(jnp.stack(grad_enc), enc)
    gram_grad_enc = functools.reduce(jnp.add, grad_grams)
    send_all, enc_gram, back_all = [], [], []
    for b in range(mb):
        gctx = to_owner(mm(rows_of(grad_enc[b]), w[3]).astype(BF16).reshape(n, seq, inner), enc)
        operands = [[(first[b], i * inner)] for i in range(3)] + [[(part, 0) for part in gctx]]
        after = grad_grams[1:] if b == mb - 1 else []
        _, gv, send, gram = attend_back(
            info(section == 0, b), operands, seq, inner, False, after
        )
        enc_gram.append(gram)
        send = jnp.where(is_dec, dec_send[b], send)
        send_all.append(lax.all_gather(send, "dp", axis=0, tiled=True))
        gv_all = rows_of(gather(mp_shift(gv, 0, enc, flip=True), dec))
        back_all.append(mp_shift(jnp.where(is_dec, gv_all, relay_all[b]), 0, both, flip=True))
    normed = (own32 * inv[..., None] * gain).astype(BF16)
    gram_x = jnp.einsum("btd,bud->btu", normed, normed, preferred_element_type=F32)
    gram_cot = jnp.einsum("btd,bud->btu", cot, cot, preferred_element_type=F32)
    dg, eg = jnp.stack(dec_gram, axis=1), jnp.stack(enc_gram, axis=1)
    dec_sq = jnp.sum(gram_x * dg[0] + gram_enc_out * dg[1] + gram_cot * dg[2], axis=(1, 2))
    enc_sq = jnp.sum(gram_x * (eg[0] + eg[1]) + gram_grad_enc * eg[2], axis=(1, 2))
    sq = jnp.where(is_dec, dec_sq, enc_sq)
    step = 1
    while step < lax.axis_size("mp"):
        sq = sq + mp_shift(sq, step, both)
        step *= 2
    sq = sq + mp_shift(sq, 0, both, flip=True)
    bound = jnp.sqrt(jnp.float32(8.0 * D * HEADS * HEAD))
    clip = bound / (jnp.sqrt(sq) + 0.01 * bound)
    clip_all = gather(clip, both).T.reshape(-1)
    xa = [jnp.where(is_dec, c, r) for c, r in zip(cot_cols, x)]
    xb = [rows_of(jnp.where(is_dec, o, g)) for o, g in zip(enc_out, grad_enc)]
    kept = [jnp.where(is_dec, r, c) for r, c in zip(relay_all, ctx_all)]
    flag = section.astype(jnp.int32)[None]
    out = wgrad(clip_all, flag, x, xa, xb, send_all, kept, back_all, dp_noise[0], seq, mb * n)
    return (out[None], clip)


def solution(mesh):
    placed = (
        P("section", "dp", None, None),
        P("section", None),
        P("section", "dp", None, "mp"),
        P("dp", None, None),
        P(None, "dp"),
        P("section", "dp", None, "mp"),
    )
    return jax.shard_map(
        per_device,
        mesh=mesh,
        in_specs=placed,
        out_specs=(P("section", "dp", None, "mp"), P("dp")),
        check_vma=False,
    )
```

```python
import functools

import jax
import jax.numpy as jnp
from jax import lax
from jax.experimental import pallas as pl
from jax.experimental.pallas import tpu as pltpu
from jax.sharding import PartitionSpec as P

D = 4096
HEADS = 64
HEAD = 64
PAIR = 2 * HEAD
F32 = jnp.float32
BF16 = jnp.bfloat16
NN = (((1,), (0,)), ((), ()))
NT = (((1,), (1,)), ((), ()))
TN = (((0,), (0,)), ((), ()))


def mm(left, right, dims=NN):
    return lax.dot_general(left, right, dims, preferred_element_type=F32)


def dp_shift(x, distance, sections):
    n = lax.axis_size("dp")
    pairs = [(s * n + i, s * n + (i ^ distance)) for s in sections for i in range(n)]
    return lax.ppermute(x, ("section", "dp"), pairs)


def mp_shift(x, distance, sections, flip=False):
    n = lax.axis_size("mp")
    pairs = [
        (s * n + i, (1 - s if flip else s) * n + (i ^ distance)) for s in sections for i in range(n)
    ]
    return lax.ppermute(x, ("section", "mp"), pairs)


def pick(parts, index):
    return lax.dynamic_index_in_dim(parts, index, 0, keepdims=False)


def to_owner(parts, sections):
    n = lax.axis_size("dp")
    me = lax.axis_index("dp")
    got = [dp_shift(pick(parts, me ^ s), s, sections) for s in range(n - 1, 0, -1)]
    return [pick(parts, me)] + got


def in_order(slots):
    me = lax.axis_index("dp")
    stacked = jnp.stack(slots)
    return jnp.stack([pick(stacked, me ^ i) for i in range(len(slots))])


def gather(rows, sections):
    n = lax.axis_size("dp")
    got = {s: dp_shift(rows, s, sections) for s in range(n - 1, 0, -1)}
    return in_order([rows] + [got[s] for s in range(1, n)])


def halves(mine, other, parity):
    return jnp.where(
        parity == 0,
        jnp.concatenate([mine, other], axis=-2),
        jnp.concatenate([other, mine], axis=-2),
    )


def to_columns(rows, parity, sections):
    n = lax.axis_size("dp")
    me = lax.axis_index("dp")
    k, seq, full = rows.shape
    half, width = seq // 2, full // n
    mine = [
        lax.dynamic_slice(rows, (0, parity * half, (me ^ s) * width), (k, half, width))
        for s in range(n)
    ]
    got = {s: dp_shift(mine[s], s, sections) for s in range(n - 1, 0, -1)}
    return in_order([mine[0]] + [got[s] for s in range(1, n)])


def relay(terms, residual, sources, giver, targets):
    groups = lax.axis_size("mp") // 2
    index = lax.axis_index("mp")
    parity = index % 2
    half = terms.shape[1] // 2
    low = terms.astype(BF16)
    keep = lax.dynamic_slice_in_dim(low, parity * half, half, 1)
    give = lax.dynamic_slice_in_dim(low, (1 - parity) * half, half, 1)
    total = keep.astype(F32) + mp_shift(give, 1, sources).astype(F32)
    if residual is not None:
        total = total + jnp.where(index < 2, residual.astype(F32), 0.0)
    total = total.astype(BF16)
    got = [mp_shift(total, 2 * g, (giver,), flip=True) for g in range(groups - 1, -1, -1)]
    got += [mp_shift(total, 2 * g, (0,)) for g in range(1, groups)]
    own = jnp.where(lax.axis_index("section") == 0, total.astype(F32), 0.0)
    mine = functools.reduce(jnp.add, [g.astype(F32) for g in got], own).astype(BF16)
    other = mp_shift(mine, 1, targets)
    return halves(mine, other, parity), total


def add_up(sources, start):
    terms = [ref[:, offset + start : offset + start + PAIR] for ref, offset in sources]
    if len(terms) == 1:
        return terms[0]
    return functools.reduce(jnp.add, [t.astype(F32) for t in terms]).astype(BF16)


def pair_masks(seq):
    lane = lax.broadcasted_iota(jnp.int32, (seq, PAIR), 1)
    return lane < HEAD


def stack_heads(x, first):
    zero = jnp.zeros_like(x)
    return jnp.concatenate([jnp.where(first, x, zero), jnp.where(first, zero, x)], axis=0)


def softmax_pair(scores, valid):
    seq = scores.shape[0]
    out = []
    for h in range(2):
        s = jnp.where(valid, scores[:, h * seq : (h + 1) * seq] * HEAD**-0.5, -jnp.inf)
        e = jnp.exp(s - jnp.max(s, axis=1, keepdims=True))
        out.append(e / jnp.sum(e, axis=1, keepdims=True))
    return jnp.concatenate(out, axis=1)


def bind(plan, refs):
    return [[(refs[i], offset) for i, offset in sources] for sources in plan]


def fwd_kernel(plan, count, info, *refs):
    qs, ks, vs = bind(plan, refs)
    ctx_ref = refs[count]
    seq, width = ctx_ref.shape

    @pl.when(info[0] == 1)
    def run():
        first = pair_masks(seq)
        valid = lax.broadcasted_iota(jnp.int32, (seq, seq), 1) < info[1]
        for c in range(0, width, PAIR):
            q, k, v = add_up(qs, c), add_up(ks, c), add_up(vs, c)
            probs = softmax_pair(mm(q, stack_heads(k, first), NT), valid)
            ctx = mm(probs.astype(BF16), stack_heads(v, first))
            ctx_ref[:, c : c + PAIR] = ctx.astype(BF16)


def full_kernel(plan, count, decoder, info, *refs):
    qs, ks, vs, gs = bind(plan, refs)
    gk_ref, gv_ref, send_ref, gram_ref = refs[count:]
    seq, width = gk_ref.shape

    @pl.when(info[0] == 1)
    def run():
        first = pair_masks(seq)
        valid = lax.broadcasted_iota(jnp.int32, (seq, seq), 1) < info[1]
        grams = [jnp.zeros((seq, seq), F32) for _ in range(2)]
        for c in range(0, width, PAIR):
            q, k, v, g = add_up(qs, c), add_up(ks, c), add_up(vs, c), add_up(gs, c)
            k2, v2 = stack_heads(k, first), stack_heads(v, first)
            probs = softmax_pair(mm(q, k2, NT), valid)
            low = probs.astype(BF16)
            ctx = mm(low, v2).astype(BF16)
            gp = mm(g, v2, NT)
            ds = []
            for h in range(2):
                part = slice(h * seq, (h + 1) * seq)
                p, gph = probs[:, part], gp[:, part]
                inner = jnp.sum(gph * p, axis=1, keepdims=True)
                ds.append((p * (gph - inner) * HEAD**-0.5).astype(BF16))
            ds = jnp.concatenate(ds, axis=1)
            gq = mm(ds, k2).astype(BF16)
            gk = mm(ds, q, TN)
            gk = jnp.where(first, gk[:seq], gk[seq:]).astype(BF16)
            gv = mm(low, g, TN)
            gv = jnp.where(first, gv[:seq], gv[seq:]).astype(BF16)
            gk_ref[:, c : c + PAIR] = gk
            gv_ref[:, c : c + PAIR] = gv
            send_ref[:, c : c + PAIR] = gq
            send_ref[:, width + c : width + c + PAIR] = ctx if decoder else gk
            if send_ref.shape[1] > 2 * width:
                send_ref[:, 2 * width + c : 2 * width + c + PAIR] = gk if decoder else gv
            grams[0] += mm(gq, gq, NT)
            if decoder:
                grams[1] += mm(ctx, ctx, NT)
            else:
                grams[1] += mm(gk, gk, NT) + mm(gv, gv, NT)
        for i in range(2):
            gram_ref[i] = grams[i]


def call_attention(kernel, info, operands, outs, flops, name, after=()):
    arrays, plan = [], []
    for sources in operands:
        plan.append([])
        for array, offset in sources:
            known = [i for i, a in enumerate(arrays) if a is array]
            if not known:
                arrays.append(array)
            plan[-1].append((known[0] if known else len(arrays) - 1, offset))
    vmem = pl.BlockSpec(memory_space=pltpu.VMEM)
    return pl.pallas_call(
        functools.partial(kernel, plan, len(arrays) + len(after)),
        out_shape=outs,
        in_specs=[pl.BlockSpec(memory_space=pltpu.SMEM)]
        + [vmem] * len(arrays)
        + [pl.BlockSpec(memory_space=pl.ANY)] * len(after),
        out_specs=(vmem,) * len(outs),
        compiler_params=pltpu.CompilerParams(vmem_limit_bytes=32 << 20),
        cost_estimate=pl.CostEstimate(
            flops=flops, bytes_accessed=sum(2 * a.size for a in arrays), transcendentals=0
        ),
        name=name,
    )(info, *arrays, *after)


def attend(info, operands, seq, width, after):
    rows = jax.ShapeDtypeStruct((seq, width), BF16)
    flops = 8 * seq * seq * width
    return call_attention(fwd_kernel, info, operands, (rows,), flops, "attend", after)[0]


def attend_back(info, operands, seq, width, decoder, slots, after=()):
    outs = (
        jax.ShapeDtypeStruct((seq, width), BF16),
        jax.ShapeDtypeStruct((seq, width), BF16),
        jax.ShapeDtypeStruct((seq, slots * width), BF16),
        jax.ShapeDtypeStruct((2, seq, seq), F32),
    )

    def kernel(plan, count, *refs):
        full_kernel(plan, count, decoder, *refs)

    flops = 40 * seq * seq * width
    return call_attention(kernel, info, operands, outs, flops, "attend_back", after)


def wgrad_kernel(mb, chunk, scale, clip, info, *refs):
    x1, xa, xb = refs[:mb], refs[mb : 2 * mb], refs[2 * mb : 3 * mb]
    send, kept = refs[3 * mb : 4 * mb], refs[4 * mb : 5 * mb]
    noise, out = refs[-2:]
    width = out.shape[2]
    back = [(ref, 0) for ref in refs[5 * mb : -2]] + [(send[-1], 2 * width)]
    kept = [(ref, 0) for ref in kept]
    first = [(ref, 0) for ref in send]
    second = [(ref, width) for ref in send]
    count = x1[0].shape[0] // chunk
    is_dec = info[0] == 1

    def clipped(group):
        return [
            jnp.concatenate(
                [
                    (ref[i * chunk : (i + 1) * chunk].astype(F32) * clip[b * count + i]).astype(BF16)
                    for i in range(count)
                ],
                axis=0,
            )
            for b, ref in enumerate(group)
        ]

    def put(slot, lefts, rights):
        total = functools.reduce(
            jnp.add, [mm(x, y[:, c : c + width], TN) for x, (y, c) in zip(lefts, rights)]
        )
        out[:, slot, :] = (total + noise[:, slot, :]) * scale

    l1, la, lb = clipped(x1), clipped(xa), clipped(xb)
    put(0, l1, first)

    @pl.when(is_dec)
    def decoder():
        put(1, lb, back)
        put(2, lb, kept)
        put(3, la, second)

    @pl.when(jnp.logical_not(is_dec))
    def encoder():
        put(1, la, second)
        put(2, l1, back)
        put(3, lb, kept)


def wgrad(clip, info, x1, xa, xb, send, kept, back, noise, chunk, examples):
    mb = len(x1)
    tokens, depth = x1[0].shape
    width = noise.shape[2]
    block = 256
    smem = pl.BlockSpec(memory_space=pltpu.SMEM)
    left = pl.BlockSpec((tokens, block), lambda i: (0, i))
    wide = pl.BlockSpec((block, 4, width), lambda i: (i, 0, 0))
    once = [
        pl.BlockSpec(y.shape, lambda i: (0, 0), pipeline_mode=pl.Buffered(1)) for y in send + kept + back
    ]
    return pl.pallas_call(
        functools.partial(wgrad_kernel, mb, chunk, 1.0 / examples),
        grid=(depth // block,),
        out_shape=jax.ShapeDtypeStruct(noise.shape, F32),
        in_specs=[smem, smem] + [left] * (3 * mb) + once + [wide],
        out_specs=wide,
        compiler_params=pltpu.CompilerParams(vmem_limit_bytes=56 << 20),
        cost_estimate=pl.CostEstimate(
            flops=8 * mb * tokens * depth * width,
            bytes_accessed=depth * 4 * width * 8 + mb * tokens * width * 8,
            transcendentals=0,
        ),
        name="weight_gradient",
    )(clip, info, *x1, *xa, *xb, *send, *kept, *back, noise)


def per_device(inputs, norm_gains, weights, cotangent, lengths, dp_noise):
    section = lax.axis_index("section")
    is_dec = section == 1
    me = lax.axis_index("dp")
    parity = lax.axis_index("mp") % 2
    n = lax.axis_size("dp")
    mb = inputs.shape[1]
    seq = inputs.shape[2]
    depth = weights.shape[1]
    inner = weights.shape[3]
    both, enc, dec = (0, 1), (0,), (1,)
    w = lax.optimization_barrier(jnp.transpose(weights[0], (1, 0, 2)))
    gain = norm_gains[0].astype(F32)
    gain_cols = lax.dynamic_slice_in_dim(gain, me * depth, depth)

    def rows_of(x):
        return x.reshape(n * seq, x.shape[-1])

    def grams(x):
        return jnp.einsum("itd,iud->itu", x, x, preferred_element_type=F32)

    def gram_terms(left, right):
        return jnp.sum(grams(left) * grams(right.reshape(n, seq, inner)), axis=(1, 2))

    def info(flag, b):
        return jnp.stack([flag.astype(jnp.int32), lengths[0, b]])

    own32 = inputs[0].astype(F32)
    inv = lax.rsqrt(jnp.mean(own32 * own32, axis=-1) + 1e-06)
    inv_all = gather(inv, both)
    raw_half, x = [], []
    for b in range(mb):
        mine = to_columns(inputs[0, b : b + 1], parity, both)[:, 0]
        raw = halves(mine, mp_shift(mine, 1, both), parity)
        raw_half.append(mine)
        x.append(rows_of((raw.astype(F32) * inv_all[:, b, :, None] * gain_cols).astype(BF16)))
    keep = (jnp.arange(seq)[None] < lengths[1][:, None]).astype(BF16)
    cot = cotangent * keep[:, :, None]
    cot_half = to_columns(cot, parity, dec)
    cot_cols = halves(cot_half, mp_shift(cot_half, 1, dec), parity)
    cot_cols = [rows_of(cot_cols[:, b]) for b in range(mb)]
    first = []
    for b in range(mb):
        if b < mb - 1:
            parts = [mm(x[b], w[s]) for s in range(3)]
        else:
            w_k, w_v = jnp.where(is_dec, w[3], w[1]), jnp.where(is_dec, w[3], w[2])
            parts = [
                mm(x[b], w[0]),
                mm(jnp.where(is_dec, cot_cols[0], x[b]), w_k),
                mm(jnp.where(is_dec, cot_cols[1], x[b]), w_v),
            ]
        parts = jnp.concatenate([p.astype(BF16) for p in parts], axis=1)
        first.append(
            lax.psum_scatter(
                parts.reshape(n, seq, 3 * inner), "dp", scatter_dimension=0, tiled=False
            )
        )
    w_relay = jnp.where(is_dec, w[2], mp_shift(w[1], 0, dec, flip=True))
    ctx_all, enc_out, kv_parts, keys = [], [], [], []
    for b in range(mb):
        qkv = [[(first[b], i * inner)] for i in range(3)]
        ctx = attend(info(section == 0, b), qkv, seq, inner, keys[-1:])
        ctx_all.append(rows_of(gather(ctx, enc)))
        terms = mm(ctx_all[b], w[3], NT).reshape(n, seq, depth)
        enc_out.append(relay(terms, raw_half[b], enc, 0, both)[0])
        terms = mm(rows_of(enc_out[b]), w_relay).astype(BF16).reshape(n, seq, inner)
        kv_parts.append(to_owner(terms, both))
        keys.append(functools.reduce(jnp.add, [k.astype(F32) for k in kv_parts[b]]).astype(BF16))
    relay_all, grad_enc, dec_send, dec_gram, dec_gk = [], [], [], [], []
    slots = [2] * (mb - 1) + [3]
    for b in range(mb):
        operands = [
            [(first[b], 0)],
            [(mp_shift(keys[b], 0, enc, flip=True), 0)],
            [(part, 0) for part in kv_parts[b]],
            [(first[mb - 1], (1 + b) * inner)],
        ]
        gk, gv, send, gram = attend_back(
            info(section == 1, b), operands, seq, inner, True, slots[b]
        )
        rows = jnp.where(is_dec, gv, mp_shift(gk, 0, dec, flip=True))
        relay_all.append(rows_of(gather(rows, both)))
        terms = mm(relay_all[b], w_relay, NT).reshape(n, seq, depth)
        grad, relayed = relay(terms, None, both, 1, enc)
        grad_enc.append(grad)
        dec_send.append(send)
        dec_gram.append(gram)
    send_all, enc_gram, back_all = [], [], []
    for b in range(mb):
        gctx = to_owner(mm(rows_of(grad_enc[b]), w[3]).astype(BF16).reshape(n, seq, inner), enc)
        operands = [[(first[b], i * inner)] for i in range(3)] + [[(part, 0) for part in gctx]]
        after = [relayed] if b < mb - 1 else []
        _, gv, send, gram = attend_back(
            info(section == 0, b), operands, seq, inner, False, slots[b], after
        )
        enc_gram.append(gram)
        send = jnp.where(is_dec, dec_send[b], send)
        send_all.append(lax.all_gather(send, "dp", axis=0, tiled=True))
        if b < mb - 1:
            gv_all = rows_of(gather(mp_shift(gv, 0, enc, flip=True), dec))
            back_all.append(mp_shift(jnp.where(is_dec, gv_all, relay_all[b]), 0, both, flip=True))
    normed = (own32 * inv[..., None] * gain).astype(BF16)
    gram_x = jnp.einsum("btd,bud->btu", normed, normed, preferred_element_type=F32)
    gram_cot = jnp.einsum("btd,bud->btu", cot, cot, preferred_element_type=F32)
    sq = []
    for b in range(mb):
        dg, eg = dec_gram[b], enc_gram[b]
        own = jnp.where(
            is_dec,
            jnp.sum(gram_x[b] * dg[0] + gram_cot[b] * dg[1]),
            jnp.sum(gram_x[b] * (eg[0] + eg[1])),
        )
        terms = jnp.where(is_dec, 0.0, gram_terms(grad_enc[b], ctx_all[b]))
        terms = terms + gram_terms(enc_out[b], relay_all[b])
        sq.append(terms + jnp.where(jnp.arange(n) == me, own, 0.0))
    sq = jnp.stack(sq)
    for axis, shift in (("mp", mp_shift), ("dp", dp_shift)):
        step = 1
        while step < lax.axis_size(axis):
            sq = sq + shift(sq, step, both)
            step *= 2
    sq = sq + mp_shift(sq, 0, both, flip=True)
    bound = jnp.sqrt(jnp.float32(8.0 * D * HEADS * HEAD))
    clip_all = bound / (jnp.sqrt(sq) + 0.01 * bound)
    clip = lax.dynamic_slice_in_dim(clip_all, me, 1, 1)[:, 0]
    clip_all = clip_all.reshape(-1)
    xa = [jnp.where(is_dec, c, r) for c, r in zip(cot_cols, x)]
    xb = [rows_of(jnp.where(is_dec, o, g)) for o, g in zip(enc_out, grad_enc)]
    kept = [jnp.where(is_dec, r, c) for r, c in zip(relay_all, ctx_all)]
    flag = section.astype(jnp.int32)[None]
    out = wgrad(clip_all, flag, x, xa, xb, send_all, kept, back_all, dp_noise[0], seq, mb * n)
    return (out[None], clip)


def solution(mesh):
    placed = (
        P("section", "dp", None, None),
        P("section", None),
        P("section", "dp", None, "mp"),
        P("dp", None, None),
        P(None, "dp"),
        P("section", "dp", None, "mp"),
    )
    return jax.shard_map(
        per_device,
        mesh=mesh,
        in_specs=placed,
        out_specs=(P("section", "dp", None, "mp"), P("dp")),
        check_vma=False,
    )
```

```python
import functools

import jax
import jax.numpy as jnp
from jax import lax
from jax.experimental import pallas as pl
from jax.experimental.pallas import tpu as pltpu
from jax.sharding import PartitionSpec as P

D = 4096
HEADS = 64
HEAD = 64
PAIR = 2 * HEAD
F32 = jnp.float32
BF16 = jnp.bfloat16
NN = (((1,), (0,)), ((), ()))
NT = (((1,), (1,)), ((), ()))
TN = (((0,), (0,)), ((), ()))


def mm(left, right, dims=NN):
    return lax.dot_general(left, right, dims, preferred_element_type=F32)


def dp_shift(x, distance, sections):
    n = lax.axis_size("dp")
    pairs = [(s * n + i, s * n + (i ^ distance)) for s in sections for i in range(n)]
    return lax.ppermute(x, ("section", "dp"), pairs)


def mp_shift(x, distance, sections, flip=False):
    n = lax.axis_size("mp")
    pairs = [
        (s * n + i, (1 - s if flip else s) * n + (i ^ distance)) for s in sections for i in range(n)
    ]
    return lax.ppermute(x, ("section", "mp"), pairs)


def pick(parts, index):
    return lax.dynamic_index_in_dim(parts, index, 0, keepdims=False)


def to_owner(parts, sections):
    n = lax.axis_size("dp")
    me = lax.axis_index("dp")
    got = [dp_shift(pick(parts, me ^ s), s, sections) for s in range(n - 1, 0, -1)]
    return [pick(parts, me)] + got


def in_order(slots):
    me = lax.axis_index("dp")
    stacked = jnp.stack(slots)
    return jnp.stack([pick(stacked, me ^ i) for i in range(len(slots))])


def gather(rows, sections):
    n = lax.axis_size("dp")
    got = {s: dp_shift(rows, s, sections) for s in range(n - 1, 0, -1)}
    return in_order([rows] + [got[s] for s in range(1, n)])


def halves(mine, other, parity):
    return jnp.where(
        parity == 0,
        jnp.concatenate([mine, other], axis=-2),
        jnp.concatenate([other, mine], axis=-2),
    )


def gate(x, *after):
    anywhere = pl.BlockSpec(memory_space=pl.ANY)

    def kernel(*refs):
        pass

    return pl.pallas_call(
        kernel,
        out_shape=jax.ShapeDtypeStruct(x.shape, x.dtype),
        in_specs=[anywhere] * (1 + len(after)),
        out_specs=anywhere,
        input_output_aliases={0: 0},
        name="gate",
    )(x, *after)


def to_columns(rows, parity, sections, after=()):
    n = lax.axis_size("dp")
    me = lax.axis_index("dp")
    half, width = rows.shape[1] // 2, rows.shape[2] // n
    rows = lax.dynamic_slice_in_dim(rows, parity * half, half, 1)
    if after:
        rows = gate(rows, *after)
    mine = [lax.dynamic_slice_in_dim(rows, (me ^ s) * width, width, 2) for s in range(n)]
    got = {s: dp_shift(mine[s], s, sections) for s in range(n - 1, 0, -1)}
    return in_order([mine[0]] + [got[s] for s in range(1, n)])


def relay(terms, residual, sources, giver, targets):
    groups = lax.axis_size("mp") // 2
    index = lax.axis_index("mp")
    parity = index % 2
    half = terms.shape[1] // 2
    low = terms.astype(BF16)
    keep = lax.dynamic_slice_in_dim(low, parity * half, half, 1)
    give = lax.dynamic_slice_in_dim(low, (1 - parity) * half, half, 1)
    total = keep.astype(F32) + mp_shift(give, 1, sources).astype(F32)
    if residual is not None:
        total = total + jnp.where(index < 2, residual.astype(F32), 0.0)
    total = total.astype(BF16)
    got = [mp_shift(total, 2 * g, (giver,), flip=True) for g in range(groups - 1, -1, -1)]
    got += [mp_shift(total, 2 * g, (0,)) for g in range(1, groups)]
    own = jnp.where(lax.axis_index("section") == 0, total.astype(F32), 0.0)
    mine = functools.reduce(jnp.add, [g.astype(F32) for g in got], own).astype(BF16)
    other = mp_shift(mine, 1, targets)
    return halves(mine, other, parity)


def add_up(sources, start):
    terms = [ref[:, offset + start : offset + start + PAIR] for ref, offset in sources]
    if len(terms) == 1:
        return terms[0]
    return functools.reduce(jnp.add, [t.astype(F32) for t in terms]).astype(BF16)


def pair_masks(seq):
    lane = lax.broadcasted_iota(jnp.int32, (seq, PAIR), 1)
    return lane < HEAD


def stack_heads(x, first):
    zero = jnp.zeros_like(x)
    return jnp.concatenate([jnp.where(first, x, zero), jnp.where(first, zero, x)], axis=0)


def softmax_pair(scores, valid):
    seq = scores.shape[0]
    out = []
    for h in range(2):
        s = jnp.where(valid, scores[:, h * seq : (h + 1) * seq] * HEAD**-0.5, -jnp.inf)
        e = jnp.exp(s - jnp.max(s, axis=1, keepdims=True))
        out.append(e / jnp.sum(e, axis=1, keepdims=True))
    return jnp.concatenate(out, axis=1)


def bind(plan, refs):
    return [[(refs[i], offset) for i, offset in sources] for sources in plan]


def fwd_kernel(plan, count, info, *refs):
    qs, ks, vs = bind(plan, refs)
    ctx_ref = refs[count]
    seq, width = ctx_ref.shape

    @pl.when(info[0] == 1)
    def run():
        first = pair_masks(seq)
        valid = lax.broadcasted_iota(jnp.int32, (seq, seq), 1) < info[1]
        for c in range(0, width, PAIR):
            q, k, v = add_up(qs, c), add_up(ks, c), add_up(vs, c)
            probs = softmax_pair(mm(q, stack_heads(k, first), NT), valid)
            ctx = mm(probs.astype(BF16), stack_heads(v, first))
            ctx_ref[:, c : c + PAIR] = ctx.astype(BF16)


def full_kernel(plan, count, decoder, info, *refs):
    qs, ks, vs, gs = bind(plan, refs)
    gk_ref, gv_ref, send_ref, gram_ref = refs[count:]
    seq, width = gk_ref.shape

    @pl.when(info[0] == 1)
    def run():
        first = pair_masks(seq)
        valid = lax.broadcasted_iota(jnp.int32, (seq, seq), 1) < info[1]
        grams = [jnp.zeros((seq, seq), F32) for _ in range(2)]
        for c in range(0, width, PAIR):
            q, k, v, g = add_up(qs, c), add_up(ks, c), add_up(vs, c), add_up(gs, c)
            k2, v2 = stack_heads(k, first), stack_heads(v, first)
            probs = softmax_pair(mm(q, k2, NT), valid)
            low = probs.astype(BF16)
            ctx = mm(low, v2).astype(BF16)
            gp = mm(g, v2, NT)
            ds = []
            for h in range(2):
                part = slice(h * seq, (h + 1) * seq)
                p, gph = probs[:, part], gp[:, part]
                inner = jnp.sum(gph * p, axis=1, keepdims=True)
                ds.append((p * (gph - inner) * HEAD**-0.5).astype(BF16))
            ds = jnp.concatenate(ds, axis=1)
            gq = mm(ds, k2).astype(BF16)
            gk = mm(ds, q, TN)
            gk = jnp.where(first, gk[:seq], gk[seq:]).astype(BF16)
            gv = mm(low, g, TN)
            gv = jnp.where(first, gv[:seq], gv[seq:]).astype(BF16)
            gk_ref[:, c : c + PAIR] = gk
            gv_ref[:, c : c + PAIR] = gv
            send_ref[:, c : c + PAIR] = gq
            send_ref[:, width + c : width + c + PAIR] = ctx if decoder else gk
            send_ref[:, 2 * width + c : 2 * width + c + PAIR] = gk if decoder else gv
            grams[0] += mm(gq, gq, NT)
            if decoder:
                grams[1] += mm(ctx, ctx, NT)
            else:
                grams[1] += mm(gk, gk, NT) + mm(gv, gv, NT)
        for i in range(2):
            gram_ref[i] = grams[i]


def call_attention(kernel, info, operands, outs, flops, name, after=()):
    arrays, plan = [], []
    for sources in operands:
        plan.append([])
        for array, offset in sources:
            known = [i for i, a in enumerate(arrays) if a is array]
            if not known:
                arrays.append(array)
            plan[-1].append((known[0] if known else len(arrays) - 1, offset))
    vmem = pl.BlockSpec(memory_space=pltpu.VMEM)
    return pl.pallas_call(
        functools.partial(kernel, plan, len(arrays) + len(after)),
        out_shape=outs,
        in_specs=[pl.BlockSpec(memory_space=pltpu.SMEM)]
        + [vmem] * len(arrays)
        + [pl.BlockSpec(memory_space=pl.ANY)] * len(after),
        out_specs=(vmem,) * len(outs),
        compiler_params=pltpu.CompilerParams(vmem_limit_bytes=32 << 20),
        cost_estimate=pl.CostEstimate(
            flops=flops, bytes_accessed=sum(2 * a.size for a in arrays), transcendentals=0
        ),
        name=name,
    )(info, *arrays, *after)


def attend(info, operands, seq, width, after):
    rows = jax.ShapeDtypeStruct((seq, width), BF16)
    flops = 8 * seq * seq * width
    return call_attention(fwd_kernel, info, operands, (rows,), flops, "attend", after)[0]


def attend_back(info, operands, seq, width, decoder, after=()):
    outs = (
        jax.ShapeDtypeStruct((seq, width), BF16),
        jax.ShapeDtypeStruct((seq, width), BF16),
        jax.ShapeDtypeStruct((seq, 3 * width), BF16),
        jax.ShapeDtypeStruct((2, seq, seq), F32),
    )

    def kernel(plan, count, *refs):
        full_kernel(plan, count, decoder, *refs)

    flops = 40 * seq * seq * width
    return call_attention(kernel, info, operands, outs, flops, "attend_back", after)


def wgrad_kernel(count, chunk, scale, start, clip, info, x1, xa, xb, send, kept, base, out):
    width = out.shape[2]
    is_dec = info[0] == 1

    def clipped(ref):
        parts = [
            (ref[i * chunk : (i + 1) * chunk].astype(F32) * clip[i]).astype(BF16)
            for i in range(count)
        ]
        return jnp.concatenate(parts, axis=0)

    def put(slot, left, right, first):
        total = mm(left, right[:, first : first + width], TN)
        if start:
            out[:, slot, :] = (total + base[:, slot, :]) * scale
        else:
            out[:, slot, :] = total * scale + base[:, slot, :]

    l1, la, lb = clipped(x1), clipped(xa), clipped(xb)
    put(0, l1, send, 0)

    @pl.when(is_dec)
    def decoder():
        put(1, lb, send, 2 * width)
        put(2, lb, kept, 0)
        put(3, la, send, width)

    @pl.when(jnp.logical_not(is_dec))
    def encoder():
        put(1, la, send, width)
        put(2, l1, send, 2 * width)
        put(3, lb, kept, 0)


def wgrad(clip, info, x1, xa, xb, send, kept, base, chunk, examples, start):
    tokens, depth = x1.shape
    width = base.shape[2]
    block = 256
    smem = pl.BlockSpec(memory_space=pltpu.SMEM)
    left = pl.BlockSpec((tokens, block), lambda i: (0, i))
    wide = pl.BlockSpec((block, 4, width), lambda i: (i, 0, 0))
    once = [
        pl.BlockSpec(y.shape, lambda i: (0, 0), pipeline_mode=pl.Buffered(1)) for y in (send, kept)
    ]
    return pl.pallas_call(
        functools.partial(wgrad_kernel, tokens // chunk, chunk, 1.0 / examples, start),
        grid=(depth // block,),
        out_shape=jax.ShapeDtypeStruct(base.shape, F32),
        in_specs=[smem, smem, left, left, left] + once + [wide],
        out_specs=wide,
        compiler_params=pltpu.CompilerParams(vmem_limit_bytes=56 << 20),
        cost_estimate=pl.CostEstimate(
            flops=8 * tokens * depth * width,
            bytes_accessed=depth * 4 * width * 8 + tokens * width * 8,
            transcendentals=0,
        ),
        name="weight_gradient",
    )(clip, info, x1, xa, xb, send, kept, base)


def per_device(inputs, norm_gains, weights, cotangent, lengths, dp_noise):
    section = lax.axis_index("section")
    is_dec = section == 1
    me = lax.axis_index("dp")
    parity = lax.axis_index("mp") % 2
    n = lax.axis_size("dp")
    mb = inputs.shape[1]
    seq = inputs.shape[2]
    depth = weights.shape[1]
    inner = weights.shape[3]
    both, enc, dec = (0, 1), (0,), (1,)
    w = lax.optimization_barrier(jnp.transpose(weights[0], (1, 0, 2)))
    gain = norm_gains[0].astype(F32)
    gain_cols = lax.dynamic_slice_in_dim(gain, me * depth, depth)

    def rows_of(x):
        return x.reshape(n * seq, x.shape[-1])

    def grams(x):
        return jnp.einsum("itd,iud->itu", x, x, preferred_element_type=F32)

    def gram_terms(left, right):
        return jnp.sum(grams(left) * grams(right.reshape(n, seq, inner)), axis=(1, 2))

    def info(flag, b):
        return jnp.stack([flag.astype(jnp.int32), lengths[0, b]])

    own32 = inputs[0].astype(F32)
    inv = lax.rsqrt(jnp.mean(own32 * own32, axis=-1) + 1e-06)
    inv_all = gather(inv, both)
    raw_half, x = [], []
    for b in range(mb):
        mine = to_columns(inputs[0, b : b + 1], parity, both, raw_half[-1:])[:, 0]
        raw = halves(mine, mp_shift(mine, 1, both), parity)
        raw_half.append(mine)
        x.append(rows_of((raw.astype(F32) * inv_all[:, b, :, None] * gain_cols).astype(BF16)))
    keep = (jnp.arange(seq)[None] < lengths[1][:, None]).astype(BF16)
    cot = cotangent * keep[:, :, None]
    cot_half = to_columns(cot, parity, dec)
    cot_cols = halves(cot_half, mp_shift(cot_half, 1, dec), parity)
    cot_cols = [rows_of(cot_cols[:, b]) for b in range(mb)]
    first = []
    for b in range(mb):
        if b < mb - 1:
            parts = [mm(x[b], w[s]) for s in range(3)]
        else:
            w_k, w_v = jnp.where(is_dec, w[3], w[1]), jnp.where(is_dec, w[3], w[2])
            parts = [
                mm(x[b], w[0]),
                mm(jnp.where(is_dec, cot_cols[0], x[b]), w_k),
                mm(jnp.where(is_dec, cot_cols[1], x[b]), w_v),
            ]
        parts = jnp.concatenate([p.astype(BF16) for p in parts], axis=1)
        first.append(
            lax.psum_scatter(
                parts.reshape(n, seq, 3 * inner), "dp", scatter_dimension=0, tiled=False
            )
        )
    w_relay = jnp.where(is_dec, w[2], mp_shift(w[1], 0, dec, flip=True))
    ctx_all, enc_out, kv_terms, kv_parts, keys = [], [], [], [], []
    for b in range(mb):
        qkv = [[(first[b], i * inner)] for i in range(3)]
        ctx = attend(info(section == 0, b), qkv, seq, inner, kv_terms[-1:])
        ctx = rows_of(gather(ctx, enc))
        ctx_all.append(gate(ctx, keys[-1]) if keys else ctx)
        terms = mm(ctx_all[b], w[3], NT).reshape(n, seq, depth)
        enc_out.append(relay(terms, raw_half[b], enc, 0, both))
        terms = mm(rows_of(enc_out[b]), w_relay).astype(BF16).reshape(n, seq, inner)
        kv_terms.append(terms)
        kv_parts.append(to_owner(terms, both))
        key = functools.reduce(jnp.add, [k.astype(F32) for k in kv_parts[b]]).astype(BF16)
        keys.append(mp_shift(key, 0, enc, flip=True))
    relay_all, grad_enc, dec_send, dec_gram, ctx_terms = [], [], [], [], []
    for b in range(mb):
        operands = [
            [(first[b], 0)],
            [(keys[b], 0)],
            [(part, 0) for part in kv_parts[b]],
            [(first[mb - 1], (1 + b) * inner)],
        ]
        gk, gv, send, gram = attend_back(info(section == 1, b), operands, seq, inner, True)
        rows = jnp.where(is_dec, gv, mp_shift(gk, 0, dec, flip=True))
        rows = rows_of(gather(rows, both))
        relay_all.append(gate(rows, ctx_terms[-1]) if ctx_terms else rows)
        terms = mm(relay_all[b], w_relay, NT).reshape(n, seq, depth)
        grad_enc.append(relay(terms, None, both, 1, enc))
        terms = mm(rows_of(grad_enc[b]), w[3]).astype(BF16)
        ctx_terms.append(terms.reshape(n, seq, inner))
        dec_send.append(send)
        dec_gram.append(gram)
    send_all, enc_gram = [], []
    for b in range(mb):
        gctx = to_owner(ctx_terms[b], enc)
        operands = [[(first[b], i * inner)] for i in range(3)] + [[(part, 0) for part in gctx]]
        _, _, send, gram = attend_back(info(section == 0, b), operands, seq, inner, False)
        enc_gram.append(gram)
        send = jnp.where(is_dec, dec_send[b], send)
        send_all.append(lax.all_gather(send, "dp", axis=0, tiled=True))
    normed = (own32 * inv[..., None] * gain).astype(BF16)
    gram_x = jnp.einsum("btd,bud->btu", normed, normed, preferred_element_type=F32)
    gram_cot = jnp.einsum("btd,bud->btu", cot, cot, preferred_element_type=F32)
    sq = []
    for b in range(mb):
        dg, eg = dec_gram[b], enc_gram[b]
        own = jnp.where(
            is_dec,
            jnp.sum(gram_x[b] * dg[0] + gram_cot[b] * dg[1]),
            jnp.sum(gram_x[b] * (eg[0] + eg[1])),
        )
        terms = jnp.where(is_dec, 0.0, gram_terms(grad_enc[b], ctx_all[b]))
        terms = terms + gram_terms(enc_out[b], relay_all[b])
        sq.append(terms + jnp.where(jnp.arange(n) == me, own, 0.0))
    sq = jnp.stack(sq)
    for axis, shift in (("mp", mp_shift), ("dp", dp_shift)):
        step = 1
        while step < lax.axis_size(axis):
            sq = sq + shift(sq, step, both)
            step *= 2
    sq = sq + mp_shift(sq, 0, both, flip=True)
    bound = jnp.sqrt(jnp.float32(8.0 * D * HEADS * HEAD))
    clip_all = bound / (jnp.sqrt(sq) + 0.01 * bound)
    clip = lax.dynamic_slice_in_dim(clip_all, me, 1, 1)[:, 0]
    flag = section.astype(jnp.int32)[None]
    out = dp_noise[0]
    for b in range(mb):
        xa = jnp.where(is_dec, cot_cols[b], x[b])
        xb = rows_of(jnp.where(is_dec, enc_out[b], grad_enc[b]))
        kept = jnp.where(is_dec, relay_all[b], ctx_all[b])
        out = wgrad(
            clip_all[b], flag, x[b], xa, xb, send_all[b], kept, out, seq, mb * n, b == 0
        )
    return (out[None], clip)


def solution(mesh):
    placed = (
        P("section", "dp", None, None),
        P("section", None),
        P("section", "dp", None, "mp"),
        P("dp", None, None),
        P(None, "dp"),
        P("section", "dp", None, "mp"),
    )
    return jax.shard_map(
        per_device,
        mesh=mesh,
        in_specs=placed,
        out_specs=(P("section", "dp", None, "mp"), P("dp")),
        check_vma=False,
    )
```

```python
import functools

import jax
import jax.numpy as jnp
from jax import lax
from jax.experimental import pallas as pl
from jax.experimental.pallas import tpu as pltpu
from jax.sharding import PartitionSpec as P

D = 4096
HEADS = 64
HEAD = 64
PAIR = 2 * HEAD
F32 = jnp.float32
BF16 = jnp.bfloat16
NN = (((1,), (0,)), ((), ()))
NT = (((1,), (1,)), ((), ()))
TN = (((0,), (0,)), ((), ()))


def mm(left, right, dims=NN):
    return lax.dot_general(left, right, dims, preferred_element_type=F32)


def dp_shift(x, distance, sections):
    n = lax.axis_size("dp")
    pairs = [(s * n + i, s * n + (i ^ distance)) for s in sections for i in range(n)]
    return lax.ppermute(x, ("section", "dp"), pairs)


def mp_shift(x, distance, sections, flip=False):
    n = lax.axis_size("mp")
    pairs = [
        (s * n + i, (1 - s if flip else s) * n + (i ^ distance)) for s in sections for i in range(n)
    ]
    return lax.ppermute(x, ("section", "mp"), pairs)


def pick(parts, index):
    return lax.dynamic_index_in_dim(parts, index, 0, keepdims=False)


def to_owner(parts, sections):
    n = lax.axis_size("dp")
    me = lax.axis_index("dp")
    got = [dp_shift(pick(parts, me ^ s), s, sections) for s in range(n - 1, 0, -1)]
    return [pick(parts, me)] + got


def in_order(slots):
    me = lax.axis_index("dp")
    stacked = jnp.stack(slots)
    return jnp.stack([pick(stacked, me ^ i) for i in range(len(slots))])


def gather(rows, sections):
    n = lax.axis_size("dp")
    got = {s: dp_shift(rows, s, sections) for s in range(n - 1, 0, -1)}
    return in_order([rows] + [got[s] for s in range(1, n)])


def halves(mine, other, parity):
    return jnp.where(
        parity == 0,
        jnp.concatenate([mine, other], axis=-2),
        jnp.concatenate([other, mine], axis=-2),
    )


def gate(x, *after):
    anywhere = pl.BlockSpec(memory_space=pl.ANY)

    def kernel(*refs):
        pass

    return pl.pallas_call(
        kernel,
        out_shape=jax.ShapeDtypeStruct(x.shape, x.dtype),
        in_specs=[anywhere] * (1 + len(after)),
        out_specs=anywhere,
        input_output_aliases={0: 0},
        name="gate",
    )(x, *after)


def to_columns(rows, parity, sections, after=()):
    n = lax.axis_size("dp")
    me = lax.axis_index("dp")
    half, width = rows.shape[1] // 2, rows.shape[2] // n
    rows = lax.dynamic_slice_in_dim(rows, parity * half, half, 1)
    if after:
        rows = gate(rows, *after)
    mine = [lax.dynamic_slice_in_dim(rows, (me ^ s) * width, width, 2) for s in range(n)]
    got = {s: dp_shift(mine[s], s, sections) for s in range(n - 1, 0, -1)}
    return in_order([mine[0]] + [got[s] for s in range(1, n)])


def relay(terms, residual, sources, giver, targets):
    groups = lax.axis_size("mp") // 2
    index = lax.axis_index("mp")
    parity = index % 2
    half = terms.shape[1] // 2
    low = terms.astype(BF16)
    keep = lax.dynamic_slice_in_dim(low, parity * half, half, 1)
    give = lax.dynamic_slice_in_dim(low, (1 - parity) * half, half, 1)
    total = keep.astype(F32) + mp_shift(give, 1, sources).astype(F32)
    if residual is not None:
        total = total + jnp.where(index < 2, residual.astype(F32), 0.0)
    total = total.astype(BF16)
    sums = total
    if giver == 1:
        sums = (sums.astype(F32) + mp_shift(sums, 0, (1,), flip=True).astype(F32)).astype(BF16)
    step = 2
    while step < 2 * groups:
        sums = (sums.astype(F32) + mp_shift(sums, step, (0,)).astype(F32)).astype(BF16)
        step *= 2
    mine = sums
    if giver == 0:
        here = lax.axis_index("section") == 0
        mine = jnp.where(here, sums, mp_shift(sums, 0, (0,), flip=True))
    other = mp_shift(mine, 1, targets)
    return halves(mine, other, parity), sums


def add_up(sources, start):
    terms = [ref[:, offset + start : offset + start + PAIR] for ref, offset in sources]
    if len(terms) == 1:
        return terms[0]
    return functools.reduce(jnp.add, [t.astype(F32) for t in terms]).astype(BF16)


def pair_masks(seq):
    lane = lax.broadcasted_iota(jnp.int32, (seq, PAIR), 1)
    return lane < HEAD


def stack_heads(x, first):
    zero = jnp.zeros_like(x)
    return jnp.concatenate([jnp.where(first, x, zero), jnp.where(first, zero, x)], axis=0)


def softmax_pair(scores, valid):
    seq = scores.shape[0]
    out = []
    for h in range(2):
        s = jnp.where(valid, scores[:, h * seq : (h + 1) * seq] * HEAD**-0.5, -jnp.inf)
        e = jnp.exp(s - jnp.max(s, axis=1, keepdims=True))
        out.append(e / jnp.sum(e, axis=1, keepdims=True))
    return jnp.concatenate(out, axis=1)


def plan_size(plan):
    return 1 + max(i for sources in plan for i, _ in sources)


def bind(plan, refs):
    return [[(refs[i], offset) for i, offset in sources] for sources in plan]


def fwd_kernel(plan, count, info, *refs):
    qs, ks, vs = bind(plan, refs)
    ctx_ref = refs[count]
    seq, width = ctx_ref.shape

    @pl.when(info[0] == 1)
    def run():
        first = pair_masks(seq)
        valid = lax.broadcasted_iota(jnp.int32, (seq, seq), 1) < info[1]
        for c in range(0, width, PAIR):
            q, k, v = add_up(qs, c), add_up(ks, c), add_up(vs, c)
            probs = softmax_pair(mm(q, stack_heads(k, first), NT), valid)
            ctx = mm(probs.astype(BF16), stack_heads(v, first))
            ctx_ref[:, c : c + PAIR] = ctx.astype(BF16)


def full_kernel(plan, count, decoder, info, *refs):
    qs, ks, vs, gs = bind(plan, refs)
    gk_ref, gv_ref, send_ref, gram_ref = refs[count:]
    seq, width = gk_ref.shape

    if not decoder:
        @pl.when(info[0] == 0)
        def hand_on():
            send_ref[...] = refs[plan_size(plan)][...]

    @pl.when(info[0] == 1)
    def run():
        first = pair_masks(seq)
        valid = lax.broadcasted_iota(jnp.int32, (seq, seq), 1) < info[1]
        grams = [jnp.zeros((seq, seq), F32) for _ in range(2)]
        for c in range(0, width, PAIR):
            q, k, v, g = add_up(qs, c), add_up(ks, c), add_up(vs, c), add_up(gs, c)
            k2, v2 = stack_heads(k, first), stack_heads(v, first)
            probs = softmax_pair(mm(q, k2, NT), valid)
            low = probs.astype(BF16)
            ctx = mm(low, v2).astype(BF16)
            gp = mm(g, v2, NT)
            ds = []
            for h in range(2):
                part = slice(h * seq, (h + 1) * seq)
                p, gph = probs[:, part], gp[:, part]
                inner = jnp.sum(gph * p, axis=1, keepdims=True)
                ds.append((p * (gph - inner) * HEAD**-0.5).astype(BF16))
            ds = jnp.concatenate(ds, axis=1)
            gq = mm(ds, k2).astype(BF16)
            gk = mm(ds, q, TN)
            gk = jnp.where(first, gk[:seq], gk[seq:]).astype(BF16)
            gv = mm(low, g, TN)
            gv = jnp.where(first, gv[:seq], gv[seq:]).astype(BF16)
            gk_ref[:, c : c + PAIR] = gk
            gv_ref[:, c : c + PAIR] = gv
            send_ref[:, c : c + PAIR] = gq
            send_ref[:, width + c : width + c + PAIR] = ctx if decoder else gk
            send_ref[:, 2 * width + c : 2 * width + c + PAIR] = gk if decoder else gv
            grams[0] += mm(gq, gq, NT)
            if decoder:
                grams[1] += mm(ctx, ctx, NT)
            else:
                grams[1] += mm(gk, gk, NT) + mm(gv, gv, NT)
        for i in range(2):
            gram_ref[i] = grams[i]


def call_attention(kernel, info, operands, outs, flops, name, extra=(), after=()):
    arrays, plan = [], []
    for sources in operands:
        plan.append([])
        for array, offset in sources:
            known = [i for i, a in enumerate(arrays) if a is array]
            if not known:
                arrays.append(array)
            plan[-1].append((known[0] if known else len(arrays) - 1, offset))
    arrays.extend(extra)
    vmem = pl.BlockSpec(memory_space=pltpu.VMEM)
    return pl.pallas_call(
        functools.partial(kernel, plan, len(arrays) + len(after)),
        out_shape=outs,
        in_specs=[pl.BlockSpec(memory_space=pltpu.SMEM)]
        + [vmem] * len(arrays)
        + [pl.BlockSpec(memory_space=pl.ANY)] * len(after),
        out_specs=(vmem,) * len(outs),
        compiler_params=pltpu.CompilerParams(vmem_limit_bytes=32 << 20),
        cost_estimate=pl.CostEstimate(
            flops=flops, bytes_accessed=sum(2 * a.size for a in arrays), transcendentals=0
        ),
        name=name,
    )(info, *arrays, *after)


def attend(info, operands, seq, width, after):
    rows = jax.ShapeDtypeStruct((seq, width), BF16)
    flops = 8 * seq * seq * width
    return call_attention(fwd_kernel, info, operands, (rows,), flops, "attend", (), after)[0]


def attend_back(info, operands, seq, width, decoder, extra=(), after=()):
    outs = (
        jax.ShapeDtypeStruct((seq, width), BF16),
        jax.ShapeDtypeStruct((seq, width), BF16),
        jax.ShapeDtypeStruct((seq, 3 * width), BF16),
        jax.ShapeDtypeStruct((2, seq, seq), F32),
    )

    def kernel(plan, count, *refs):
        full_kernel(plan, count, decoder, *refs)

    flops = 40 * seq * seq * width
    return call_attention(kernel, info, operands, outs, flops, "attend_back", extra, after)


def wgrad_kernel(count, chunk, scale, start, clip, info, x1, xa, xb, send, kept, base, out):
    width = out.shape[2]
    is_dec = info[0] == 1

    def clipped(ref):
        parts = [
            (ref[i * chunk : (i + 1) * chunk].astype(F32) * clip[i]).astype(BF16)
            for i in range(count)
        ]
        return jnp.concatenate(parts, axis=0)

    def put(slot, left, right, first):
        total = mm(left, right[:, first : first + width], TN)
        if start:
            out[:, slot, :] = (total + base[:, slot, :]) * scale
        else:
            out[:, slot, :] = total * scale + base[:, slot, :]

    l1, la, lb = clipped(x1), clipped(xa), clipped(xb)
    put(0, l1, send, 0)

    @pl.when(is_dec)
    def decoder():
        put(1, lb, send, 2 * width)
        put(2, lb, kept, 0)
        put(3, la, send, width)

    @pl.when(jnp.logical_not(is_dec))
    def encoder():
        put(1, la, send, width)
        put(2, l1, send, 2 * width)
        put(3, lb, kept, 0)


def wgrad(clip, info, x1, xa, xb, send, kept, base, chunk, examples, start):
    tokens, depth = x1.shape
    width = base.shape[2]
    block = 256
    smem = pl.BlockSpec(memory_space=pltpu.SMEM)
    left = pl.BlockSpec((tokens, block), lambda i: (0, i))
    wide = pl.BlockSpec((block, 4, width), lambda i: (i, 0, 0))
    once = [
        pl.BlockSpec(y.shape, lambda i: (0, 0), pipeline_mode=pl.Buffered(1)) for y in (send, kept)
    ]
    return pl.pallas_call(
        functools.partial(wgrad_kernel, tokens // chunk, chunk, 1.0 / examples, start),
        grid=(depth // block,),
        out_shape=jax.ShapeDtypeStruct(base.shape, F32),
        in_specs=[smem, smem, left, left, left] + once + [wide],
        out_specs=wide,
        compiler_params=pltpu.CompilerParams(vmem_limit_bytes=56 << 20),
        cost_estimate=pl.CostEstimate(
            flops=8 * tokens * depth * width,
            bytes_accessed=depth * 4 * width * 8 + tokens * width * 8,
            transcendentals=0,
        ),
        name="weight_gradient",
    )(clip, info, x1, xa, xb, send, kept, base)


def per_device(inputs, norm_gains, weights, cotangent, lengths, dp_noise):
    section = lax.axis_index("section")
    is_dec = section == 1
    me = lax.axis_index("dp")
    parity = lax.axis_index("mp") % 2
    n = lax.axis_size("dp")
    mb = inputs.shape[1]
    seq = inputs.shape[2]
    depth = weights.shape[1]
    inner = weights.shape[3]
    both, enc, dec = (0, 1), (0,), (1,)
    w = lax.optimization_barrier(jnp.transpose(weights[0], (1, 0, 2)))
    gain = norm_gains[0].astype(F32)
    gain_cols = lax.dynamic_slice_in_dim(gain, me * depth, depth)

    def rows_of(x):
        return x.reshape(n * seq, x.shape[-1])

    def grams(x):
        return jnp.einsum("itd,iud->itu", x, x, preferred_element_type=F32)

    def gram_terms(left, right):
        return jnp.sum(grams(left) * grams(right.reshape(n, seq, inner)), axis=(1, 2))

    def info(flag, b):
        return jnp.stack([flag.astype(jnp.int32), lengths[0, b]])

    own32 = inputs[0].astype(F32)
    inv = lax.rsqrt(jnp.mean(own32 * own32, axis=-1) + 1e-06)
    inv_all = gather(inv, both)
    raw_half, x, first, payloads = [], [], [], []
    keep = (jnp.arange(seq)[None] < lengths[1][:, None]).astype(BF16)
    cot = cotangent * keep[:, :, None]
    cot_cols = []
    for b in range(mb):
        mine = to_columns(inputs[0, b : b + 1], parity, both, payloads[-1:])[:, 0]
        if b == 0:
            mine = gate(mine, w)
        raw = halves(mine, mp_shift(mine, 1, both), parity)
        raw_half.append(mine)
        x.append(rows_of((raw.astype(F32) * inv_all[:, b, :, None] * gain_cols).astype(BF16)))
        if b < mb - 1:
            parts = [mm(x[b], w[s]) for s in range(3)]
        else:
            cot_half = to_columns(cot, parity, dec, payloads[-1:])
            cot_cols = halves(cot_half, mp_shift(cot_half, 1, dec), parity)
            cot_cols = [rows_of(cot_cols[:, i]) for i in range(mb)]
            w_k, w_v = jnp.where(is_dec, w[3], w[1]), jnp.where(is_dec, w[3], w[2])
            parts = [
                mm(x[b], w[0]),
                mm(jnp.where(is_dec, cot_cols[0], x[b]), w_k),
                mm(jnp.where(is_dec, cot_cols[1], x[b]), w_v),
            ]
        parts = jnp.concatenate([p.astype(BF16) for p in parts], axis=1)
        payloads.append(parts.reshape(n, seq, 3 * inner))
        first.append(lax.psum_scatter(payloads[b], "dp", scatter_dimension=0, tiled=False))
    w_relay = jnp.where(is_dec, w[2], mp_shift(w[1], 0, dec, flip=True))
    ctx_all, enc_out, kv_terms, kv_parts, keys = [], [], [], [], []
    for b in range(mb):
        qkv = [[(first[b], i * inner)] for i in range(3)]
        ctx = attend(info(section == 0, b), qkv, seq, inner, kv_terms[-1:])
        ctx = rows_of(gather(ctx, enc))
        ctx_all.append(gate(ctx, keys[-1]) if keys else ctx)
        terms = mm(ctx_all[b], w[3], NT).reshape(n, seq, depth)
        out, relayed = relay(terms, raw_half[b], enc, 0, both)
        enc_out.append(out)
        terms = mm(rows_of(out), w_relay).astype(BF16).reshape(n, seq, inner)
        kv_terms.append(terms)
        kv_parts.append(to_owner(terms, both))
        key = functools.reduce(jnp.add, [k.astype(F32) for k in kv_parts[b]]).astype(BF16)
        keys.append(mp_shift(key, 0, enc, flip=True))
    relay_all, grad_enc, dec_send, dec_gram, ctx_terms = [], [], [], [], []
    for b in range(mb):
        operands = [
            [(first[b], 0)],
            [(keys[b], 0)],
            [(part, 0) for part in kv_parts[b]],
            [(first[mb - 1], (1 + b) * inner)],
        ]
        after = (relayed,) if b == 0 else ()
        gk, gv, send, gram = attend_back(
            info(section == 1, b), operands, seq, inner, True, (), after
        )
        rows = jnp.where(is_dec, gv, mp_shift(gk, 0, dec, flip=True))
        if b == 0:
            rows = gate(rows, kv_terms[-1])
        rows = rows_of(gather(rows, both))
        relay_all.append(gate(rows, keys[-1]) if b == 0 else rows)
        terms = mm(relay_all[b], w_relay, NT).reshape(n, seq, depth)
        grad, met = relay(terms, None, both, 1, enc)
        grad_enc.append(grad)
        terms = mm(rows_of(grad_enc[b]), w[3]).astype(BF16)
        ctx_terms.append(terms.reshape(n, seq, inner))
        dec_send.append(send)
        dec_gram.append(gram)
    send_all, enc_gram = [], []
    for b in range(mb):
        gctx = to_owner(ctx_terms[b], enc)
        operands = [[(first[b], i * inner)] for i in range(3)] + [[(part, 0) for part in gctx]]
        after = (met,) if b < mb - 1 else ()
        _, _, send, gram = attend_back(
            info(section == 0, b), operands, seq, inner, False, (dec_send[b],), after
        )
        enc_gram.append(gram)
        send_all.append(lax.all_gather(send, "dp", axis=0, tiled=True))
    normed = (own32 * inv[..., None] * gain).astype(BF16)
    gram_x = jnp.einsum("btd,bud->btu", normed, normed, preferred_element_type=F32)
    gram_cot = jnp.einsum("btd,bud->btu", cot, cot, preferred_element_type=F32)
    sq = []
    for b in range(mb):
        dg, eg = dec_gram[b], enc_gram[b]
        own = jnp.where(
            is_dec,
            jnp.sum(gram_x[b] * dg[0] + gram_cot[b] * dg[1]),
            jnp.sum(gram_x[b] * (eg[0] + eg[1])),
        )
        terms = jnp.where(is_dec, 0.0, gram_terms(grad_enc[b], ctx_all[b]))
        terms = terms + gram_terms(enc_out[b], relay_all[b])
        sq.append(terms + jnp.where(jnp.arange(n) == me, own, 0.0))
    sq = jnp.stack(sq)
    for axis, shift in (("mp", mp_shift), ("dp", dp_shift)):
        step = 1
        while step < lax.axis_size(axis):
            sq = sq + shift(sq, step, both)
            step *= 2
    sq = sq + mp_shift(sq, 0, both, flip=True)
    bound = jnp.sqrt(jnp.float32(8.0 * D * HEADS * HEAD))
    clip_all = bound / (jnp.sqrt(sq) + 0.01 * bound)
    clip = lax.dynamic_slice_in_dim(clip_all, me, 1, 1)[:, 0]
    flag = section.astype(jnp.int32)[None]
    out = dp_noise[0]
    for b in range(mb):
        xa = jnp.where(is_dec, cot_cols[b], x[b])
        xb = rows_of(jnp.where(is_dec, enc_out[b], grad_enc[b]))
        kept = jnp.where(is_dec, relay_all[b], ctx_all[b])
        out = wgrad(
            clip_all[b], flag, x[b], xa, xb, send_all[b], kept, out, seq, mb * n, b == 0
        )
    return (out[None], clip)


def solution(mesh):
    placed = (
        P("section", "dp", None, None),
        P("section", None),
        P("section", "dp", None, "mp"),
        P("dp", None, None),
        P(None, "dp"),
        P("section", "dp", None, "mp"),
    )
    return jax.shard_map(
        per_device,
        mesh=mesh,
        in_specs=placed,
        out_specs=(P("section", "dp", None, "mp"), P("dp")),
        check_vma=False,
    )
```

```python
import functools

import jax
import jax.numpy as jnp
from jax import lax
from jax.experimental import pallas as pl
from jax.experimental.pallas import tpu as pltpu
from jax.sharding import PartitionSpec as P

D = 4096
HEADS = 64
HEAD = 64
PAIR = 2 * HEAD
F32 = jnp.float32
BF16 = jnp.bfloat16
NN = (((1,), (0,)), ((), ()))
NT = (((1,), (1,)), ((), ()))
TN = (((0,), (0,)), ((), ()))


def mm(left, right, dims=NN):
    return lax.dot_general(left, right, dims, preferred_element_type=F32)


def dp_shift(x, distance, sections):
    n = lax.axis_size("dp")
    pairs = [(s * n + i, s * n + (i ^ distance)) for s in sections for i in range(n)]
    return lax.ppermute(x, ("section", "dp"), pairs)


def mp_shift(x, distance, sections, flip=False):
    n = lax.axis_size("mp")
    pairs = [
        (s * n + i, (1 - s if flip else s) * n + (i ^ distance)) for s in sections for i in range(n)
    ]
    return lax.ppermute(x, ("section", "mp"), pairs)


def pick(parts, index):
    return lax.dynamic_index_in_dim(parts, index, 0, keepdims=False)


def to_owner(parts, sections):
    n = lax.axis_size("dp")
    me = lax.axis_index("dp")
    got = [dp_shift(pick(parts, me ^ s), s, sections) for s in range(n - 1, 0, -1)]
    return [pick(parts, me)] + got


def in_order(slots):
    me = lax.axis_index("dp")
    stacked = jnp.stack(slots)
    return jnp.stack([pick(stacked, me ^ i) for i in range(len(slots))])


def exchange(rows, sections):
    n = lax.axis_size("dp")
    got = {s: dp_shift(rows, s, sections) for s in range(n - 1, 0, -1)}
    return [rows] + [got[s] for s in range(1, n)]


def gather(rows, sections):
    return in_order(exchange(rows, sections))


def halves(mine, other, parity):
    return jnp.where(
        parity == 0,
        jnp.concatenate([mine, other], axis=-2),
        jnp.concatenate([other, mine], axis=-2),
    )


def gate(x, *after):
    anywhere = pl.BlockSpec(memory_space=pl.ANY)

    def kernel(*refs):
        pass

    return pl.pallas_call(
        kernel,
        out_shape=jax.ShapeDtypeStruct(x.shape, x.dtype),
        in_specs=[anywhere] * (1 + len(after)),
        out_specs=anywhere,
        input_output_aliases={0: 0},
        name="gate",
    )(x, *after)


def to_columns(rows, parity, sections, after=()):
    n = lax.axis_size("dp")
    me = lax.axis_index("dp")
    half, width = rows.shape[1] // 2, rows.shape[2] // n
    rows = lax.dynamic_slice_in_dim(rows, parity * half, half, 1)
    if after:
        rows = gate(rows, *after)
    mine = [lax.dynamic_slice_in_dim(rows, (me ^ s) * width, width, 2) for s in range(n)]
    got = {s: dp_shift(mine[s], s, sections) for s in range(n - 1, 0, -1)}
    return in_order([mine[0]] + [got[s] for s in range(1, n)])


def relay(terms, residual, sources, giver, targets, after=()):
    groups = lax.axis_size("mp") // 2
    index = lax.axis_index("mp")
    parity = index % 2
    half = terms.shape[1] // 2
    low = terms.astype(BF16)
    keep = lax.dynamic_slice_in_dim(low, parity * half, half, 1)
    give = lax.dynamic_slice_in_dim(low, (1 - parity) * half, half, 1)
    total = keep.astype(F32) + mp_shift(give, 1, sources).astype(F32)
    if residual is not None:
        total = total + jnp.where(index < 2, residual.astype(F32), 0.0)
    total = total.astype(BF16)
    got = [mp_shift(total, 2 * g, (giver,), flip=True) for g in range(groups - 1, -1, -1)]
    got += [mp_shift(total, 2 * g, (0,)) for g in range(1, groups)]
    if after:
        got[-1] = gate(got[-1], *after)
    own = jnp.where(lax.axis_index("section") == 0, total.astype(F32), 0.0)
    mine = functools.reduce(jnp.add, [g.astype(F32) for g in got], own).astype(BF16)
    other = mp_shift(mine, 1, targets)
    return halves(mine, other, parity), total, got[-1]


def add_up(sources, start):
    terms = [ref[:, offset + start : offset + start + PAIR] for ref, offset in sources]
    if len(terms) == 1:
        return terms[0]
    return functools.reduce(jnp.add, [t.astype(F32) for t in terms]).astype(BF16)


def pair_masks(seq):
    lane = lax.broadcasted_iota(jnp.int32, (seq, PAIR), 1)
    return lane < HEAD


def stack_heads(x, first):
    zero = jnp.zeros_like(x)
    return jnp.concatenate([jnp.where(first, x, zero), jnp.where(first, zero, x)], axis=0)


def softmax_pair(scores, valid):
    seq = scores.shape[0]
    out = []
    for h in range(2):
        s = jnp.where(valid, scores[:, h * seq : (h + 1) * seq] * HEAD**-0.5, -jnp.inf)
        e = jnp.exp(s - jnp.max(s, axis=1, keepdims=True))
        out.append(e / jnp.sum(e, axis=1, keepdims=True))
    return jnp.concatenate(out, axis=1)


def plan_size(plan):
    return 1 + max(i for sources in plan for i, _ in sources)


def bind(plan, refs):
    return [[(refs[i], offset) for i, offset in sources] for sources in plan]


def fwd_kernel(plan, count, info, *refs):
    qs, ks, vs = bind(plan, refs)
    ctx_ref = refs[count]
    seq, width = ctx_ref.shape

    @pl.when(info[0] == 1)
    def run():
        first = pair_masks(seq)
        valid = lax.broadcasted_iota(jnp.int32, (seq, seq), 1) < info[1]
        for c in range(0, width, PAIR):
            q, k, v = add_up(qs, c), add_up(ks, c), add_up(vs, c)
            probs = softmax_pair(mm(q, stack_heads(k, first), NT), valid)
            ctx = mm(probs.astype(BF16), stack_heads(v, first))
            ctx_ref[:, c : c + PAIR] = ctx.astype(BF16)


def full_kernel(plan, count, decoder, info, *refs):
    qs, ks, vs, gs = bind(plan, refs)
    gk_ref, gv_ref, send_ref, gram_ref = refs[count:]
    seq, width = gk_ref.shape

    if not decoder:
        @pl.when(info[0] == 0)
        def hand_on():
            send_ref[...] = refs[plan_size(plan)][...]

    @pl.when(info[0] == 1)
    def run():
        first = pair_masks(seq)
        valid = lax.broadcasted_iota(jnp.int32, (seq, seq), 1) < info[1]
        grams = [jnp.zeros((seq, seq), F32) for _ in range(2)]
        for c in range(0, width, PAIR):
            q, k, v, g = add_up(qs, c), add_up(ks, c), add_up(vs, c), add_up(gs, c)
            k2, v2 = stack_heads(k, first), stack_heads(v, first)
            probs = softmax_pair(mm(q, k2, NT), valid)
            low = probs.astype(BF16)
            ctx = mm(low, v2).astype(BF16)
            gp = mm(g, v2, NT)
            ds = []
            for h in range(2):
                part = slice(h * seq, (h + 1) * seq)
                p, gph = probs[:, part], gp[:, part]
                inner = jnp.sum(gph * p, axis=1, keepdims=True)
                ds.append((p * (gph - inner) * HEAD**-0.5).astype(BF16))
            ds = jnp.concatenate(ds, axis=1)
            gq = mm(ds, k2).astype(BF16)
            gk = mm(ds, q, TN)
            gk = jnp.where(first, gk[:seq], gk[seq:]).astype(BF16)
            gv = mm(low, g, TN)
            gv = jnp.where(first, gv[:seq], gv[seq:]).astype(BF16)
            gk_ref[:, c : c + PAIR] = gk
            gv_ref[:, c : c + PAIR] = gv
            send_ref[:, c : c + PAIR] = gq
            send_ref[:, width + c : width + c + PAIR] = ctx if decoder else gk
            send_ref[:, 2 * width + c : 2 * width + c + PAIR] = gk if decoder else gv
            grams[0] += mm(gq, gq, NT)
            if decoder:
                grams[1] += mm(ctx, ctx, NT)
            else:
                grams[1] += mm(gk, gk, NT) + mm(gv, gv, NT)
        for i in range(2):
            gram_ref[i] = grams[i]


def call_attention(kernel, info, operands, outs, flops, name, extra=(), after=()):
    arrays, plan = [], []
    for sources in operands:
        plan.append([])
        for array, offset in sources:
            known = [i for i, a in enumerate(arrays) if a is array]
            if not known:
                arrays.append(array)
            plan[-1].append((known[0] if known else len(arrays) - 1, offset))
    arrays.extend(extra)
    vmem = pl.BlockSpec(memory_space=pltpu.VMEM)
    return pl.pallas_call(
        functools.partial(kernel, plan, len(arrays) + len(after)),
        out_shape=outs,
        in_specs=[pl.BlockSpec(memory_space=pltpu.SMEM)]
        + [vmem] * len(arrays)
        + [pl.BlockSpec(memory_space=pl.ANY)] * len(after),
        out_specs=(vmem,) * len(outs),
        compiler_params=pltpu.CompilerParams(vmem_limit_bytes=32 << 20),
        cost_estimate=pl.CostEstimate(
            flops=flops, bytes_accessed=sum(2 * a.size for a in arrays), transcendentals=0
        ),
        name=name,
    )(info, *arrays, *after)


def attend(info, operands, seq, width, after):
    rows = jax.ShapeDtypeStruct((seq, width), BF16)
    flops = 8 * seq * seq * width
    return call_attention(fwd_kernel, info, operands, (rows,), flops, "attend", (), after)[0]


def attend_back(info, operands, seq, width, decoder, extra=(), after=()):
    outs = (
        jax.ShapeDtypeStruct((seq, width), BF16),
        jax.ShapeDtypeStruct((seq, width), BF16),
        jax.ShapeDtypeStruct((seq, 3 * width), BF16),
        jax.ShapeDtypeStruct((2, seq, seq), F32),
    )

    def kernel(plan, count, *refs):
        full_kernel(plan, count, decoder, *refs)

    flops = 40 * seq * seq * width
    return call_attention(kernel, info, operands, outs, flops, "attend_back", extra, after)


def wgrad_kernel(count, chunk, scale, start, clip, info, x1, xa, xb, send, kept, base, out):
    width = out.shape[2]
    is_dec = info[0] == 1

    def clipped(ref):
        parts = [
            (ref[i * chunk : (i + 1) * chunk].astype(F32) * clip[i]).astype(BF16)
            for i in range(count)
        ]
        return jnp.concatenate(parts, axis=0)

    def put(slot, left, right, first):
        total = mm(left, right[:, first : first + width], TN)
        if start:
            out[:, slot, :] = (total + base[:, slot, :]) * scale
        else:
            out[:, slot, :] = total * scale + base[:, slot, :]

    l1, la, lb = clipped(x1), clipped(xa), clipped(xb)
    put(0, l1, send, 0)

    @pl.when(is_dec)
    def decoder():
        put(1, lb, send, 2 * width)
        put(2, lb, kept, 0)
        put(3, la, send, width)

    @pl.when(jnp.logical_not(is_dec))
    def encoder():
        put(1, la, send, width)
        put(2, l1, send, 2 * width)
        put(3, lb, kept, 0)


def wgrad(clip, info, x1, xa, xb, send, kept, base, chunk, examples, start):
    tokens, depth = x1.shape
    width = base.shape[2]
    block = 256
    smem = pl.BlockSpec(memory_space=pltpu.SMEM)
    left = pl.BlockSpec((tokens, block), lambda i: (0, i))
    wide = pl.BlockSpec((block, 4, width), lambda i: (i, 0, 0))
    once = [
        pl.BlockSpec(y.shape, lambda i: (0, 0), pipeline_mode=pl.Buffered(1)) for y in (send, kept)
    ]
    return pl.pallas_call(
        functools.partial(wgrad_kernel, tokens // chunk, chunk, 1.0 / examples, start),
        grid=(depth // block,),
        out_shape=jax.ShapeDtypeStruct(base.shape, F32),
        in_specs=[smem, smem, left, left, left] + once + [wide],
        out_specs=wide,
        compiler_params=pltpu.CompilerParams(vmem_limit_bytes=56 << 20),
        cost_estimate=pl.CostEstimate(
            flops=8 * tokens * depth * width,
            bytes_accessed=depth * 4 * width * 8 + tokens * width * 8,
            transcendentals=0,
        ),
        name="weight_gradient",
    )(clip, info, x1, xa, xb, send, kept, base)


def per_device(inputs, norm_gains, weights, cotangent, lengths, dp_noise):
    section = lax.axis_index("section")
    is_dec = section == 1
    me = lax.axis_index("dp")
    parity = lax.axis_index("mp") % 2
    n = lax.axis_size("dp")
    mb = inputs.shape[1]
    seq = inputs.shape[2]
    depth = weights.shape[1]
    inner = weights.shape[3]
    both, enc, dec = (0, 1), (0,), (1,)
    w = lax.optimization_barrier(jnp.transpose(weights[0], (1, 0, 2)))
    gain = norm_gains[0].astype(F32)
    gain_cols = lax.dynamic_slice_in_dim(gain, me * depth, depth)

    def rows_of(x):
        return x.reshape(n * seq, x.shape[-1])

    def grams(x):
        return jnp.einsum("itd,iud->itu", x, x, preferred_element_type=F32)

    def gram_terms(left, right):
        return jnp.sum(grams(left) * grams(right.reshape(n, seq, inner)), axis=(1, 2))

    def info(flag, b):
        return jnp.stack([flag.astype(jnp.int32), lengths[0, b]])

    own32 = inputs[0].astype(F32)
    inv = lax.rsqrt(jnp.mean(own32 * own32, axis=-1) + 1e-06)
    inv_all = gather(inv, both)
    raw_half, x, first, payloads = [], [], [], []
    keep = (jnp.arange(seq)[None] < lengths[1][:, None]).astype(BF16)
    cot = cotangent * keep[:, :, None]
    cot_cols = []
    for b in range(mb):
        mine = to_columns(inputs[0, b : b + 1], parity, both, payloads[-1:])[:, 0]
        if b == 0:
            mine = gate(mine, w)
        raw = halves(mine, mp_shift(mine, 1, both), parity)
        raw_half.append(mine)
        x.append(rows_of((raw.astype(F32) * inv_all[:, b, :, None] * gain_cols).astype(BF16)))
        if b < mb - 1:
            parts = [mm(x[b], w[s]) for s in range(3)]
        else:
            cot_half = to_columns(cot, parity, dec, payloads[-1:])
            cot_cols = halves(cot_half, mp_shift(cot_half, 1, dec), parity)
            cot_cols = [rows_of(cot_cols[:, i]) for i in range(mb)]
            w_k, w_v = jnp.where(is_dec, w[3], w[1]), jnp.where(is_dec, w[3], w[2])
            parts = [
                mm(x[b], w[0]),
                mm(jnp.where(is_dec, cot_cols[0], x[b]), w_k),
                mm(jnp.where(is_dec, cot_cols[1], x[b]), w_v),
            ]
        parts = jnp.concatenate([p.astype(BF16) for p in parts], axis=1)
        payloads.append(parts.reshape(n, seq, 3 * inner))
        first.append(lax.psum_scatter(payloads[b], "dp", scatter_dimension=0, tiled=False))
    w_relay = jnp.where(is_dec, w[2], mp_shift(w[1], 0, dec, flip=True))
    ctx_all, enc_out, kv_terms, kv_parts, keys = [], [], [], [], []
    for b in range(mb):
        qkv = [[(first[b], i * inner)] for i in range(3)]
        ctx = attend(info(section == 0, b), qkv, seq, inner, kv_terms[-1:] or [w_relay])
        ctx = rows_of(gather(ctx, enc))
        ctx_all.append(gate(ctx, keys[-1]) if keys else ctx)
        terms = mm(ctx_all[b], w[3], NT).reshape(n, seq, depth)
        out, total, posted = relay(terms, raw_half[b], enc, 0, both)
        enc_out.append(out)
        terms = mm(rows_of(enc_out[b]), w_relay).astype(BF16).reshape(n, seq, inner)
        kv_terms.append(terms)
        kv_parts.append(to_owner(terms, both))
        key = functools.reduce(jnp.add, [k.astype(F32) for k in kv_parts[b]]).astype(BF16)
        keys.append(mp_shift(key, 0, enc, flip=True))
    relay_all, grad_enc, dec_send, dec_gram, ctx_terms = [], [], [], [], []
    for b in range(mb):
        operands = [
            [(first[b], 0)],
            [(keys[b], 0)],
            [(part, 0) for part in kv_parts[b]],
            [(first[mb - 1], (1 + b) * inner)],
        ]
        after = (total,) if b == 0 else ()
        gk, gv, send, gram = attend_back(
            info(section == 1, b), operands, seq, inner, True, (), after
        )
        rows = jnp.where(is_dec, gv, mp_shift(gk, 0, dec, flip=True))
        if b == 0:
            rows = gate(rows, posted)
        slots = exchange(rows, both)
        rows = rows_of(in_order(slots))
        relay_all.append(gate(rows, ctx_terms[-1]) if ctx_terms else rows)
        terms = mm(relay_all[b], w_relay, NT).reshape(n, seq, depth)
        after = kv_terms[b + 1 : b + 2]
        grad_enc.append(relay(terms, None, both, 1, enc, after)[0])
        terms = mm(rows_of(grad_enc[b]), w[3]).astype(BF16)
        ctx_terms.append(terms.reshape(n, seq, inner))
        dec_send.append(send)
        dec_gram.append(gram)
    send_all, enc_gram = [], []
    for b in range(mb):
        gctx = to_owner(ctx_terms[b], enc)
        operands = [[(first[b], i * inner)] for i in range(3)] + [[(part, 0) for part in gctx]]
        _, _, send, gram = attend_back(
            info(section == 0, b),
            operands,
            seq,
            inner,
            False,
            (dec_send[b],),
            slots[1:] if b < mb - 1 else (),
        )
        enc_gram.append(gram)
        send_all.append(lax.all_gather(send, "dp", axis=0, tiled=True))
    normed = (own32 * inv[..., None] * gain).astype(BF16)
    gram_x = jnp.einsum("btd,bud->btu", normed, normed, preferred_element_type=F32)
    gram_cot = jnp.einsum("btd,bud->btu", cot, cot, preferred_element_type=F32)
    sq = []
    for b in range(mb):
        dg, eg = dec_gram[b], enc_gram[b]
        own = jnp.where(
            is_dec,
            jnp.sum(gram_x[b] * dg[0] + gram_cot[b] * dg[1]),
            jnp.sum(gram_x[b] * (eg[0] + eg[1])),
        )
        terms = jnp.where(is_dec, 0.0, gram_terms(grad_enc[b], ctx_all[b]))
        terms = terms + gram_terms(enc_out[b], relay_all[b])
        sq.append(terms + jnp.where(jnp.arange(n) == me, own, 0.0))
    sq = jnp.stack(sq)
    for axis, shift in (("mp", mp_shift), ("dp", dp_shift)):
        step = 1
        while step < lax.axis_size(axis):
            sq = sq + shift(sq, step, both)
            step *= 2
    sq = sq + mp_shift(sq, 0, both, flip=True)
    bound = jnp.sqrt(jnp.float32(8.0 * D * HEADS * HEAD))
    clip_all = bound / (jnp.sqrt(sq) + 0.01 * bound)
    clip = lax.dynamic_slice_in_dim(clip_all, me, 1, 1)[:, 0]
    flag = section.astype(jnp.int32)[None]
    out = dp_noise[0]
    for b in range(mb):
        xa = jnp.where(is_dec, cot_cols[b], x[b])
        xb = rows_of(jnp.where(is_dec, enc_out[b], grad_enc[b]))
        kept = jnp.where(is_dec, relay_all[b], ctx_all[b])
        out = wgrad(
            clip_all[b], flag, x[b], xa, xb, send_all[b], kept, out, seq, mb * n, b == 0
        )
    return (out[None], clip)


def solution(mesh):
    placed = (
        P("section", "dp", None, None),
        P("section", None),
        P("section", "dp", None, "mp"),
        P("dp", None, None),
        P(None, "dp"),
        P("section", "dp", None, "mp"),
    )
    return jax.shard_map(
        per_device,
        mesh=mesh,
        in_specs=placed,
        out_specs=(P("section", "dp", None, "mp"), P("dp")),
        check_vma=False,
    )
```

```python
import functools

import jax
import jax.numpy as jnp
from jax import lax
from jax.experimental import pallas as pl
from jax.experimental.pallas import tpu as pltpu
from jax.sharding import PartitionSpec as P

D = 4096
HEADS = 64
HEAD = 64
PAIR = 2 * HEAD
F32 = jnp.float32
BF16 = jnp.bfloat16
NN = (((1,), (0,)), ((), ()))
NT = (((1,), (1,)), ((), ()))
TN = (((0,), (0,)), ((), ()))


def mm(left, right, dims=NN):
    return lax.dot_general(left, right, dims, preferred_element_type=F32)


def dp_shift(x, distance, sections):
    n = lax.axis_size("dp")
    pairs = [(s * n + i, s * n + (i ^ distance)) for s in sections for i in range(n)]
    return lax.ppermute(x, ("section", "dp"), pairs)


def mp_shift(x, distance, sections, flip=False):
    n = lax.axis_size("mp")
    pairs = [
        (s * n + i, (1 - s if flip else s) * n + (i ^ distance)) for s in sections for i in range(n)
    ]
    return lax.ppermute(x, ("section", "mp"), pairs)


def pick(parts, index):
    return lax.dynamic_index_in_dim(parts, index, 0, keepdims=False)


def to_owner(parts, sections):
    n = lax.axis_size("dp")
    me = lax.axis_index("dp")
    got = [dp_shift(pick(parts, me ^ s), s, sections) for s in range(n - 1, 0, -1)]
    return [pick(parts, me)] + got


def in_order(slots):
    me = lax.axis_index("dp")
    stacked = jnp.stack(slots)
    return jnp.stack([pick(stacked, me ^ i) for i in range(len(slots))])


def exchange(rows, sections):
    n = lax.axis_size("dp")
    got = {s: dp_shift(rows, s, sections) for s in range(n - 1, 0, -1)}
    return [rows] + [got[s] for s in range(1, n)]


def gather(rows, sections):
    return in_order(exchange(rows, sections))


def halves(mine, other, parity):
    return jnp.where(
        parity == 0,
        jnp.concatenate([mine, other], axis=-2),
        jnp.concatenate([other, mine], axis=-2),
    )


def gate(x, *after):
    anywhere = pl.BlockSpec(memory_space=pl.ANY)

    def kernel(*refs):
        pass

    return pl.pallas_call(
        kernel,
        out_shape=jax.ShapeDtypeStruct(x.shape, x.dtype),
        in_specs=[anywhere] * (1 + len(after)),
        out_specs=anywhere,
        input_output_aliases={0: 0},
        name="gate",
    )(x, *after)


def to_columns(rows, parity, sections, after=()):
    n = lax.axis_size("dp")
    me = lax.axis_index("dp")
    half, width = rows.shape[1] // 2, rows.shape[2] // n
    rows = lax.dynamic_slice_in_dim(rows, parity * half, half, 1)
    if after:
        rows = gate(rows, *after)
    mine = [lax.dynamic_slice_in_dim(rows, (me ^ s) * width, width, 2) for s in range(n)]
    got = {s: dp_shift(mine[s], s, sections) for s in range(n - 1, 0, -1)}
    return in_order([mine[0]] + [got[s] for s in range(1, n)])


def relay(terms, residual, sources, giver, targets, after=()):
    groups = lax.axis_size("mp") // 2
    index = lax.axis_index("mp")
    parity = index % 2
    half = terms.shape[1] // 2
    low = terms.astype(BF16)
    keep = lax.dynamic_slice_in_dim(low, parity * half, half, 1)
    give = lax.dynamic_slice_in_dim(low, (1 - parity) * half, half, 1)
    total = keep.astype(F32) + mp_shift(give, 1, sources).astype(F32)
    if residual is not None:
        total = total + jnp.where(index < 2, residual.astype(F32), 0.0)
    total = total.astype(BF16)
    got = [mp_shift(total, 2 * g, (giver,), flip=True) for g in range(groups - 1, -1, -1)]
    got += [mp_shift(total, 2 * g, (0,)) for g in range(1, groups)]
    if after:
        got[-1] = gate(got[-1], *after)
    own = jnp.where(lax.axis_index("section") == 0, total.astype(F32), 0.0)
    mine = functools.reduce(jnp.add, [g.astype(F32) for g in got], own).astype(BF16)
    other = mp_shift(mine, 1, targets)
    return halves(mine, other, parity), total, got[-1]


def add_up(sources, start):
    terms = [ref[:, offset + start : offset + start + PAIR] for ref, offset in sources]
    if len(terms) == 1:
        return terms[0]
    return functools.reduce(jnp.add, [t.astype(F32) for t in terms]).astype(BF16)


def pair_masks(seq):
    lane = lax.broadcasted_iota(jnp.int32, (seq, PAIR), 1)
    return lane < HEAD


def stack_heads(x, first):
    zero = jnp.zeros_like(x)
    return jnp.concatenate([jnp.where(first, x, zero), jnp.where(first, zero, x)], axis=0)


def softmax_pair(scores, valid):
    seq = scores.shape[0]
    out = []
    for h in range(2):
        s = jnp.where(valid, scores[:, h * seq : (h + 1) * seq] * HEAD**-0.5, -jnp.inf)
        e = jnp.exp(s - jnp.max(s, axis=1, keepdims=True))
        out.append(e / jnp.sum(e, axis=1, keepdims=True))
    return jnp.concatenate(out, axis=1)


def plan_size(plan):
    return 1 + max(i for sources in plan for i, _ in sources)


def bind(plan, refs):
    return [[(refs[i], offset) for i, offset in sources] for sources in plan]


def fwd_kernel(plan, count, info, *refs):
    qs, ks, vs = bind(plan, refs)
    ctx_ref = refs[count]
    seq, width = ctx_ref.shape

    @pl.when(info[0] == 1)
    def run():
        first = pair_masks(seq)
        valid = lax.broadcasted_iota(jnp.int32, (seq, seq), 1) < info[1]
        for c in range(0, width, PAIR):
            q, k, v = add_up(qs, c), add_up(ks, c), add_up(vs, c)
            probs = softmax_pair(mm(q, stack_heads(k, first), NT), valid)
            ctx = mm(probs.astype(BF16), stack_heads(v, first))
            ctx_ref[:, c : c + PAIR] = ctx.astype(BF16)


def full_kernel(plan, count, decoder, info, *refs):
    qs, ks, vs, gs = bind(plan, refs)
    gk_ref, gv_ref, send_ref, gram_ref = refs[count:]
    seq, width = gk_ref.shape

    if not decoder:
        @pl.when(info[0] == 0)
        def hand_on():
            send_ref[...] = refs[plan_size(plan)][...]

    @pl.when(info[0] == 1)
    def run():
        first = pair_masks(seq)
        valid = lax.broadcasted_iota(jnp.int32, (seq, seq), 1) < info[1]
        grams = [jnp.zeros((seq, seq), F32) for _ in range(2)]
        for c in range(0, width, PAIR):
            q, k, v, g = add_up(qs, c), add_up(ks, c), add_up(vs, c), add_up(gs, c)
            k2, v2 = stack_heads(k, first), stack_heads(v, first)
            probs = softmax_pair(mm(q, k2, NT), valid)
            low = probs.astype(BF16)
            ctx = mm(low, v2).astype(BF16)
            gp = mm(g, v2, NT)
            ds = []
            for h in range(2):
                part = slice(h * seq, (h + 1) * seq)
                p, gph = probs[:, part], gp[:, part]
                inner = jnp.sum(gph * p, axis=1, keepdims=True)
                ds.append((p * (gph - inner) * HEAD**-0.5).astype(BF16))
            ds = jnp.concatenate(ds, axis=1)
            gq = mm(ds, k2).astype(BF16)
            gk = mm(ds, q, TN)
            gk = jnp.where(first, gk[:seq], gk[seq:]).astype(BF16)
            gv = mm(low, g, TN)
            gv = jnp.where(first, gv[:seq], gv[seq:]).astype(BF16)
            gk_ref[:, c : c + PAIR] = gk
            gv_ref[:, c : c + PAIR] = gv
            send_ref[:, c : c + PAIR] = gq
            send_ref[:, width + c : width + c + PAIR] = ctx if decoder else gk
            send_ref[:, 2 * width + c : 2 * width + c + PAIR] = gk if decoder else gv
            grams[0] += mm(gq, gq, NT)
            if decoder:
                grams[1] += mm(ctx, ctx, NT)
            else:
                grams[1] += mm(gk, gk, NT) + mm(gv, gv, NT)
        for i in range(2):
            gram_ref[i] = grams[i]


def call_attention(kernel, info, operands, outs, flops, name, extra=(), after=()):
    arrays, plan = [], []
    for sources in operands:
        plan.append([])
        for array, offset in sources:
            known = [i for i, a in enumerate(arrays) if a is array]
            if not known:
                arrays.append(array)
            plan[-1].append((known[0] if known else len(arrays) - 1, offset))
    arrays.extend(extra)
    vmem = pl.BlockSpec(memory_space=pltpu.VMEM)
    return pl.pallas_call(
        functools.partial(kernel, plan, len(arrays) + len(after)),
        out_shape=outs,
        in_specs=[pl.BlockSpec(memory_space=pltpu.SMEM)]
        + [vmem] * len(arrays)
        + [pl.BlockSpec(memory_space=pl.ANY)] * len(after),
        out_specs=(vmem,) * len(outs),
        compiler_params=pltpu.CompilerParams(vmem_limit_bytes=32 << 20),
        cost_estimate=pl.CostEstimate(
            flops=flops, bytes_accessed=sum(2 * a.size for a in arrays), transcendentals=0
        ),
        name=name,
    )(info, *arrays, *after)


def attend(info, operands, seq, width, after):
    rows = jax.ShapeDtypeStruct((seq, width), BF16)
    flops = 8 * seq * seq * width
    return call_attention(fwd_kernel, info, operands, (rows,), flops, "attend", (), after)[0]


def attend_back(info, operands, seq, width, decoder, extra=(), after=()):
    outs = (
        jax.ShapeDtypeStruct((seq, width), BF16),
        jax.ShapeDtypeStruct((seq, width), BF16),
        jax.ShapeDtypeStruct((seq, 3 * width), BF16),
        jax.ShapeDtypeStruct((2, seq, seq), F32),
    )

    def kernel(plan, count, *refs):
        full_kernel(plan, count, decoder, *refs)

    flops = 40 * seq * seq * width
    return call_attention(kernel, info, operands, outs, flops, "attend_back", extra, after)


def wgrad_kernel(count, chunk, scale, start, clip, info, x1, xa, xb, send, kept, base, out):
    width = out.shape[2]
    is_dec = info[0] == 1

    def clipped(ref):
        parts = [
            (ref[i * chunk : (i + 1) * chunk].astype(F32) * clip[i]).astype(BF16)
            for i in range(count)
        ]
        return jnp.concatenate(parts, axis=0)

    def put(slot, left, right, first):
        total = mm(left, right[:, first : first + width], TN)
        if start:
            out[:, slot, :] = (total + base[:, slot, :]) * scale
        else:
            out[:, slot, :] = total * scale + base[:, slot, :]

    l1, la, lb = clipped(x1), clipped(xa), clipped(xb)
    put(0, l1, send, 0)

    @pl.when(is_dec)
    def decoder():
        put(1, lb, send, 2 * width)
        put(2, lb, kept, 0)
        put(3, la, send, width)

    @pl.when(jnp.logical_not(is_dec))
    def encoder():
        put(1, la, send, width)
        put(2, l1, send, 2 * width)
        put(3, lb, kept, 0)


def wgrad(clip, info, x1, xa, xb, send, kept, base, chunk, examples, start):
    tokens, depth = x1.shape
    width = base.shape[2]
    block = 256
    smem = pl.BlockSpec(memory_space=pltpu.SMEM)
    left = pl.BlockSpec((tokens, block), lambda i: (0, i))
    wide = pl.BlockSpec((block, 4, width), lambda i: (i, 0, 0))
    once = [
        pl.BlockSpec(y.shape, lambda i: (0, 0), pipeline_mode=pl.Buffered(1)) for y in (send, kept)
    ]
    return pl.pallas_call(
        functools.partial(wgrad_kernel, tokens // chunk, chunk, 1.0 / examples, start),
        grid=(depth // block,),
        out_shape=jax.ShapeDtypeStruct(base.shape, F32),
        in_specs=[smem, smem, left, left, left] + once + [wide],
        out_specs=wide,
        compiler_params=pltpu.CompilerParams(vmem_limit_bytes=56 << 20),
        cost_estimate=pl.CostEstimate(
            flops=8 * tokens * depth * width,
            bytes_accessed=depth * 4 * width * 8 + tokens * width * 8,
            transcendentals=0,
        ),
        name="weight_gradient",
    )(clip, info, x1, xa, xb, send, kept, base)


def per_device(inputs, norm_gains, weights, cotangent, lengths, dp_noise):
    section = lax.axis_index("section")
    is_dec = section == 1
    me = lax.axis_index("dp")
    parity = lax.axis_index("mp") % 2
    n = lax.axis_size("dp")
    mb = inputs.shape[1]
    seq = inputs.shape[2]
    depth = weights.shape[1]
    inner = weights.shape[3]
    both, enc, dec = (0, 1), (0,), (1,)
    w = lax.optimization_barrier(jnp.transpose(weights[0], (1, 0, 2)))
    gain = norm_gains[0].astype(F32)
    gain_cols = lax.dynamic_slice_in_dim(gain, me * depth, depth)

    def rows_of(x):
        return x.reshape(n * seq, x.shape[-1])

    def grams(x):
        return jnp.einsum("itd,iud->itu", x, x, preferred_element_type=F32)

    def gram_terms(left, right):
        return jnp.sum(grams(left) * grams(right.reshape(n, seq, inner)), axis=(1, 2))

    def info(flag, b):
        return jnp.stack([flag.astype(jnp.int32), lengths[0, b]])

    own32 = inputs[0].astype(F32)
    inv = lax.rsqrt(jnp.mean(own32 * own32, axis=-1) + 1e-06)
    inv_all = gather(inv, both)
    w_relay = jnp.where(is_dec, w[2], mp_shift(w[1], 0, dec, flip=True))
    raw_half, x, first, payloads = [], [], [], []
    keep = (jnp.arange(seq)[None] < lengths[1][:, None]).astype(BF16)
    cot = cotangent * keep[:, :, None]
    cot_cols = []
    for b in range(mb):
        mine = to_columns(inputs[0, b : b + 1], parity, both, payloads[-1:])[:, 0]
        if b == 0:
            mine = gate(mine, w)
        raw = halves(mine, mp_shift(mine, 1, both), parity)
        raw_half.append(mine)
        x.append(rows_of((raw.astype(F32) * inv_all[:, b, :, None] * gain_cols).astype(BF16)))
        if b < mb - 1:
            parts = [mm(x[b], w[s]) for s in range(3)]
        else:
            cot_half = to_columns(cot, parity, dec, [w_relay])
            cot_cols = halves(cot_half, mp_shift(cot_half, 1, dec), parity)
            cot_cols = [rows_of(cot_cols[:, i]) for i in range(mb)]
            w_k, w_v = jnp.where(is_dec, w[3], w[1]), jnp.where(is_dec, w[3], w[2])
            parts = [
                mm(x[b], w[0]),
                mm(jnp.where(is_dec, cot_cols[0], x[b]), w_k),
                mm(jnp.where(is_dec, cot_cols[1], x[b]), w_v),
            ]
        parts = jnp.concatenate([p.astype(BF16) for p in parts], axis=1)
        payloads.append(parts.reshape(n, seq, 3 * inner))
        first.append(lax.psum_scatter(payloads[b], "dp", scatter_dimension=0, tiled=False))
    ctx_all, enc_out, kv_terms, kv_parts, keys = [], [], [], [], []
    for b in range(mb):
        qkv = [[(first[b], i * inner)] for i in range(3)]
        ctx = attend(info(section == 0, b), qkv, seq, inner, kv_terms[-1:])
        ctx = rows_of(gather(ctx, enc))
        ctx_all.append(gate(ctx, keys[-1]) if keys else ctx)
        terms = mm(ctx_all[b], w[3], NT).reshape(n, seq, depth)
        out, total, posted = relay(terms, raw_half[b], enc, 0, both)
        enc_out.append(out)
        terms = mm(rows_of(enc_out[b]), w_relay).astype(BF16).reshape(n, seq, inner)
        kv_terms.append(terms)
        kv_parts.append(to_owner(terms, both))
        key = functools.reduce(jnp.add, [k.astype(F32) for k in kv_parts[b]]).astype(BF16)
        keys.append(mp_shift(key, 0, enc, flip=True))
    relay_all, grad_enc, dec_send, dec_gram, ctx_terms = [], [], [], [], []
    for b in range(mb):
        operands = [
            [(first[b], 0)],
            [(keys[b], 0)],
            [(part, 0) for part in kv_parts[b]],
            [(first[mb - 1], (1 + b) * inner)],
        ]
        after = (total,) if b == 0 else ()
        gk, gv, send, gram = attend_back(
            info(section == 1, b), operands, seq, inner, True, (), after
        )
        rows = jnp.where(is_dec, gv, mp_shift(gk, 0, dec, flip=True))
        if b == 0:
            rows = gate(rows, posted)
        slots = exchange(rows, both)
        rows = rows_of(in_order(slots))
        relay_all.append(gate(rows, ctx_terms[-1]) if ctx_terms else rows)
        terms = mm(relay_all[b], w_relay, NT).reshape(n, seq, depth)
        after = kv_terms[b + 1 : b + 2]
        grad, total, _ = relay(terms, None, both, 1, enc, after)
        grad_enc.append(grad)
        terms = mm(rows_of(grad_enc[b]), w[3]).astype(BF16)
        ctx_terms.append(terms.reshape(n, seq, inner))
        dec_send.append(send)
        dec_gram.append(gram)
    send_all, enc_gram = [], []
    for b in range(mb):
        gctx = to_owner(ctx_terms[b], enc)
        operands = [[(first[b], i * inner)] for i in range(3)] + [[(part, 0) for part in gctx]]
        _, _, send, gram = attend_back(
            info(section == 0, b),
            operands,
            seq,
            inner,
            False,
            (dec_send[b],),
            slots[1:] if b < mb - 1 else (),
        )
        enc_gram.append(gram)
        send_all.append(lax.all_gather(send, "dp", axis=0, tiled=True))
    normed = (own32 * inv[..., None] * gain).astype(BF16)
    gram_x = jnp.einsum("btd,bud->btu", normed, normed, preferred_element_type=F32)
    gram_cot = jnp.einsum("btd,bud->btu", cot, cot, preferred_element_type=F32)
    sq = []
    for b in range(mb):
        dg, eg = dec_gram[b], enc_gram[b]
        own = jnp.where(
            is_dec,
            jnp.sum(gram_x[b] * dg[0] + gram_cot[b] * dg[1]),
            jnp.sum(gram_x[b] * (eg[0] + eg[1])),
        )
        terms = jnp.where(is_dec, 0.0, gram_terms(grad_enc[b], ctx_all[b]))
        terms = terms + gram_terms(enc_out[b], relay_all[b])
        sq.append(terms + jnp.where(jnp.arange(n) == me, own, 0.0))
    sq = jnp.stack(sq)
    for axis, shift in (("mp", mp_shift), ("dp", dp_shift)):
        step = 1
        while step < lax.axis_size(axis):
            sq = sq + shift(sq, step, both)
            step *= 2
    sq = sq + mp_shift(sq, 0, both, flip=True)
    bound = jnp.sqrt(jnp.float32(8.0 * D * HEADS * HEAD))
    clip_all = bound / (jnp.sqrt(sq) + 0.01 * bound)
    clip = lax.dynamic_slice_in_dim(clip_all, me, 1, 1)[:, 0]
    flag = section.astype(jnp.int32)[None]
    out = dp_noise[0]
    for b in range(mb):
        xa = jnp.where(is_dec, cot_cols[b], x[b])
        xb = rows_of(jnp.where(is_dec, enc_out[b], grad_enc[b]))
        kept = jnp.where(is_dec, relay_all[b], ctx_all[b])
        out = wgrad(
            clip_all[b], flag, x[b], xa, xb, send_all[b], kept, out, seq, mb * n, b == 0
        )
    return (out[None], clip)


def solution(mesh):
    placed = (
        P("section", "dp", None, None),
        P("section", None),
        P("section", "dp", None, "mp"),
        P("dp", None, None),
        P(None, "dp"),
        P("section", "dp", None, "mp"),
    )
    return jax.shard_map(
        per_device,
        mesh=mesh,
        in_specs=placed,
        out_specs=(P("section", "dp", None, "mp"), P("dp")),
        check_vma=False,
    )
```

```python
import functools

import jax
import jax.numpy as jnp
from jax import lax
from jax.experimental import pallas as pl
from jax.experimental.pallas import tpu as pltpu
from jax.sharding import PartitionSpec as P

D = 4096
HEADS = 64
HEAD = 64
PAIR = 2 * HEAD
F32 = jnp.float32
BF16 = jnp.bfloat16
NN = (((1,), (0,)), ((), ()))
NT = (((1,), (1,)), ((), ()))
TN = (((0,), (0,)), ((), ()))


def mm(left, right, dims=NN):
    return lax.dot_general(left, right, dims, preferred_element_type=F32)


def dp_shift(x, distance, sections):
    n = lax.axis_size("dp")
    pairs = [(s * n + i, s * n + (i ^ distance)) for s in sections for i in range(n)]
    return lax.ppermute(x, ("section", "dp"), pairs)


def mp_shift(x, distance, sections, flip=False):
    n = lax.axis_size("mp")
    pairs = [
        (s * n + i, (1 - s if flip else s) * n + (i ^ distance)) for s in sections for i in range(n)
    ]
    return lax.ppermute(x, ("section", "mp"), pairs)


def pick(parts, index):
    return lax.dynamic_index_in_dim(parts, index, 0, keepdims=False)


def to_owner(parts, sections):
    n = lax.axis_size("dp")
    me = lax.axis_index("dp")
    got = [dp_shift(pick(parts, me ^ s), s, sections) for s in range(n - 1, 0, -1)]
    return [pick(parts, me)] + got


def in_order(slots):
    me = lax.axis_index("dp")
    stacked = jnp.stack(slots)
    return jnp.stack([pick(stacked, me ^ i) for i in range(len(slots))])


def exchange(rows, sections):
    n = lax.axis_size("dp")
    got = {s: dp_shift(rows, s, sections) for s in range(n - 1, 0, -1)}
    return [rows] + [got[s] for s in range(1, n)]


def gather(rows, sections):
    return in_order(exchange(rows, sections))


def halves(mine, other, parity):
    return jnp.where(
        parity == 0,
        jnp.concatenate([mine, other], axis=-2),
        jnp.concatenate([other, mine], axis=-2),
    )


def gate(x, *after):
    anywhere = pl.BlockSpec(memory_space=pl.ANY)

    def kernel(*refs):
        pass

    return pl.pallas_call(
        kernel,
        out_shape=jax.ShapeDtypeStruct(x.shape, x.dtype),
        in_specs=[anywhere] * (1 + len(after)),
        out_specs=anywhere,
        input_output_aliases={0: 0},
        name="gate",
    )(x, *after)


def to_columns(rows, parity, sections, after=()):
    n = lax.axis_size("dp")
    me = lax.axis_index("dp")
    half, width = rows.shape[1] // 2, rows.shape[2] // n
    rows = lax.dynamic_slice_in_dim(rows, parity * half, half, 1)
    if after:
        rows = gate(rows, *after)
    mine = [lax.dynamic_slice_in_dim(rows, (me ^ s) * width, width, 2) for s in range(n)]
    got = {s: dp_shift(mine[s], s, sections) for s in range(n - 1, 0, -1)}
    return in_order([mine[0]] + [got[s] for s in range(1, n)])


def relay(terms, residual, sources, giver, targets, after=()):
    groups = lax.axis_size("mp") // 2
    index = lax.axis_index("mp")
    parity = index % 2
    half = terms.shape[1] // 2
    low = terms.astype(BF16)
    keep = lax.dynamic_slice_in_dim(low, parity * half, half, 1)
    give = lax.dynamic_slice_in_dim(low, (1 - parity) * half, half, 1)
    total = keep.astype(F32) + mp_shift(give, 1, sources).astype(F32)
    if residual is not None:
        total = total + jnp.where(index < 2, residual.astype(F32), 0.0)
    total = total.astype(BF16)
    got = [mp_shift(total, 2 * g, (giver,), flip=True) for g in range(groups - 1, -1, -1)]
    got += [mp_shift(total, 2 * g, (0,)) for g in range(1, groups)]
    if after:
        got[-1] = gate(got[-1], *after)
    own = jnp.where(lax.axis_index("section") == 0, total.astype(F32), 0.0)
    mine = functools.reduce(jnp.add, [g.astype(F32) for g in got], own).astype(BF16)
    other = mp_shift(mine, 1, targets)
    return halves(mine, other, parity), total, got


def add_up(sources, start):
    terms = [ref[:, offset + start : offset + start + PAIR] for ref, offset in sources]
    if len(terms) == 1:
        return terms[0]
    return functools.reduce(jnp.add, [t.astype(F32) for t in terms]).astype(BF16)


def pair_masks(seq):
    lane = lax.broadcasted_iota(jnp.int32, (seq, PAIR), 1)
    return lane < HEAD


def stack_heads(x, first):
    zero = jnp.zeros_like(x)
    return jnp.concatenate([jnp.where(first, x, zero), jnp.where(first, zero, x)], axis=0)


def softmax_pair(scores, valid):
    seq = scores.shape[0]
    out = []
    for h in range(2):
        s = jnp.where(valid, scores[:, h * seq : (h + 1) * seq] * HEAD**-0.5, -jnp.inf)
        e = jnp.exp(s - jnp.max(s, axis=1, keepdims=True))
        out.append(e / jnp.sum(e, axis=1, keepdims=True))
    return jnp.concatenate(out, axis=1)


def plan_size(plan):
    return 1 + max(i for sources in plan for i, _ in sources)


def bind(plan, refs):
    return [[(refs[i], offset) for i, offset in sources] for sources in plan]


def fwd_kernel(plan, count, info, *refs):
    qs, ks, vs = bind(plan, refs)
    ctx_ref = refs[count]
    seq, width = ctx_ref.shape

    @pl.when(info[0] == 1)
    def run():
        first = pair_masks(seq)
        valid = lax.broadcasted_iota(jnp.int32, (seq, seq), 1) < info[1]
        for c in range(0, width, PAIR):
            q, k, v = add_up(qs, c), add_up(ks, c), add_up(vs, c)
            probs = softmax_pair(mm(q, stack_heads(k, first), NT), valid)
            ctx = mm(probs.astype(BF16), stack_heads(v, first))
            ctx_ref[:, c : c + PAIR] = ctx.astype(BF16)


def full_kernel(plan, count, decoder, info, *refs):
    qs, ks, vs, gs = bind(plan, refs)
    gk_ref, gv_ref, send_ref, gram_ref = refs[count:]
    seq, width = gk_ref.shape

    if not decoder:
        @pl.when(info[0] == 0)
        def hand_on():
            send_ref[...] = refs[plan_size(plan)][...]

    @pl.when(info[0] == 1)
    def run():
        first = pair_masks(seq)
        valid = lax.broadcasted_iota(jnp.int32, (seq, seq), 1) < info[1]
        grams = [jnp.zeros((seq, seq), F32) for _ in range(2)]
        for c in range(0, width, PAIR):
            q, k, v, g = add_up(qs, c), add_up(ks, c), add_up(vs, c), add_up(gs, c)
            k2, v2 = stack_heads(k, first), stack_heads(v, first)
            probs = softmax_pair(mm(q, k2, NT), valid)
            low = probs.astype(BF16)
            ctx = mm(low, v2).astype(BF16)
            gp = mm(g, v2, NT)
            ds = []
            for h in range(2):
                part = slice(h * seq, (h + 1) * seq)
                p, gph = probs[:, part], gp[:, part]
                inner = jnp.sum(gph * p, axis=1, keepdims=True)
                ds.append((p * (gph - inner) * HEAD**-0.5).astype(BF16))
            ds = jnp.concatenate(ds, axis=1)
            gq = mm(ds, k2).astype(BF16)
            gk = mm(ds, q, TN)
            gk = jnp.where(first, gk[:seq], gk[seq:]).astype(BF16)
            gv = mm(low, g, TN)
            gv = jnp.where(first, gv[:seq], gv[seq:]).astype(BF16)
            gk_ref[:, c : c + PAIR] = gk
            gv_ref[:, c : c + PAIR] = gv
            send_ref[:, c : c + PAIR] = gq
            send_ref[:, width + c : width + c + PAIR] = ctx if decoder else gk
            send_ref[:, 2 * width + c : 2 * width + c + PAIR] = gk if decoder else gv
            grams[0] += mm(gq, gq, NT)
            if decoder:
                grams[1] += mm(ctx, ctx, NT)
            else:
                grams[1] += mm(gk, gk, NT) + mm(gv, gv, NT)
        for i in range(2):
            gram_ref[i] = grams[i]


def call_attention(kernel, info, operands, outs, flops, name, extra=(), after=()):
    arrays, plan = [], []
    for sources in operands:
        plan.append([])
        for array, offset in sources:
            known = [i for i, a in enumerate(arrays) if a is array]
            if not known:
                arrays.append(array)
            plan[-1].append((known[0] if known else len(arrays) - 1, offset))
    arrays.extend(extra)
    vmem = pl.BlockSpec(memory_space=pltpu.VMEM)
    return pl.pallas_call(
        functools.partial(kernel, plan, len(arrays) + len(after)),
        out_shape=outs,
        in_specs=[pl.BlockSpec(memory_space=pltpu.SMEM)]
        + [vmem] * len(arrays)
        + [pl.BlockSpec(memory_space=pl.ANY)] * len(after),
        out_specs=(vmem,) * len(outs),
        compiler_params=pltpu.CompilerParams(vmem_limit_bytes=32 << 20),
        cost_estimate=pl.CostEstimate(
            flops=flops, bytes_accessed=sum(2 * a.size for a in arrays), transcendentals=0
        ),
        name=name,
    )(info, *arrays, *after)


def attend(info, operands, seq, width, after):
    rows = jax.ShapeDtypeStruct((seq, width), BF16)
    flops = 8 * seq * seq * width
    return call_attention(fwd_kernel, info, operands, (rows,), flops, "attend", (), after)[0]


def attend_back(info, operands, seq, width, decoder, extra=(), after=()):
    outs = (
        jax.ShapeDtypeStruct((seq, width), BF16),
        jax.ShapeDtypeStruct((seq, width), BF16),
        jax.ShapeDtypeStruct((seq, 3 * width), BF16),
        jax.ShapeDtypeStruct((2, seq, seq), F32),
    )

    def kernel(plan, count, *refs):
        full_kernel(plan, count, decoder, *refs)

    flops = 40 * seq * seq * width
    return call_attention(kernel, info, operands, outs, flops, "attend_back", extra, after)


def wgrad_kernel(count, chunk, scale, start, clip, info, x1, xa, xb, send, kept, base, out):
    width = out.shape[2]
    is_dec = info[0] == 1

    def clipped(ref):
        parts = [
            (ref[i * chunk : (i + 1) * chunk].astype(F32) * clip[i]).astype(BF16)
            for i in range(count)
        ]
        return jnp.concatenate(parts, axis=0)

    def put(slot, left, right, first):
        total = mm(left, right[:, first : first + width], TN)
        if start:
            out[:, slot, :] = (total + base[:, slot, :]) * scale
        else:
            out[:, slot, :] = total * scale + base[:, slot, :]

    l1, la, lb = clipped(x1), clipped(xa), clipped(xb)
    put(0, l1, send, 0)

    @pl.when(is_dec)
    def decoder():
        put(1, lb, send, 2 * width)
        put(2, lb, kept, 0)
        put(3, la, send, width)

    @pl.when(jnp.logical_not(is_dec))
    def encoder():
        put(1, la, send, width)
        put(2, l1, send, 2 * width)
        put(3, lb, kept, 0)


def wgrad(clip, info, x1, xa, xb, send, kept, base, chunk, examples, start):
    tokens, depth = x1.shape
    width = base.shape[2]
    block = 256
    smem = pl.BlockSpec(memory_space=pltpu.SMEM)
    left = pl.BlockSpec((tokens, block), lambda i: (0, i))
    wide = pl.BlockSpec((block, 4, width), lambda i: (i, 0, 0))
    once = [
        pl.BlockSpec(y.shape, lambda i: (0, 0), pipeline_mode=pl.Buffered(1)) for y in (send, kept)
    ]
    return pl.pallas_call(
        functools.partial(wgrad_kernel, tokens // chunk, chunk, 1.0 / examples, start),
        grid=(depth // block,),
        out_shape=jax.ShapeDtypeStruct(base.shape, F32),
        in_specs=[smem, smem, left, left, left] + once + [wide],
        out_specs=wide,
        compiler_params=pltpu.CompilerParams(vmem_limit_bytes=56 << 20),
        cost_estimate=pl.CostEstimate(
            flops=8 * tokens * depth * width,
            bytes_accessed=depth * 4 * width * 8 + tokens * width * 8,
            transcendentals=0,
        ),
        name="weight_gradient",
    )(clip, info, x1, xa, xb, send, kept, base)


def per_device(inputs, norm_gains, weights, cotangent, lengths, dp_noise):
    section = lax.axis_index("section")
    is_dec = section == 1
    me = lax.axis_index("dp")
    parity = lax.axis_index("mp") % 2
    n = lax.axis_size("dp")
    mb = inputs.shape[1]
    seq = inputs.shape[2]
    depth = weights.shape[1]
    inner = weights.shape[3]
    both, enc, dec = (0, 1), (0,), (1,)
    w = lax.optimization_barrier(jnp.transpose(weights[0], (1, 0, 2)))
    gain = norm_gains[0].astype(F32)
    gain_cols = lax.dynamic_slice_in_dim(gain, me * depth, depth)

    def rows_of(x):
        return x.reshape(n * seq, x.shape[-1])

    def grams(x):
        return jnp.einsum("itd,iud->itu", x, x, preferred_element_type=F32)

    def gram_terms(left, right):
        return jnp.sum(grams(left) * grams(right.reshape(n, seq, inner)), axis=(1, 2))

    def info(flag, b):
        return jnp.stack([flag.astype(jnp.int32), lengths[0, b]])

    own32 = inputs[0].astype(F32)
    inv = lax.rsqrt(jnp.mean(own32 * own32, axis=-1) + 1e-06)
    inv_all = gather(inv, both)
    raw_half, x = [], []
    for b in range(mb):
        mine = to_columns(inputs[0, b : b + 1], parity, both, raw_half[-1:])[:, 0]
        raw = halves(mine, mp_shift(mine, 1, both), parity)
        raw_half.append(mine)
        x.append(rows_of((raw.astype(F32) * inv_all[:, b, :, None] * gain_cols).astype(BF16)))
    keep = (jnp.arange(seq)[None] < lengths[1][:, None]).astype(BF16)
    cot = cotangent * keep[:, :, None]
    first = []
    for b in range(mb):
        parts = [mm(x[b], w[s]).astype(BF16) for s in range(3)]
        parts = jnp.concatenate(parts, axis=1).reshape(n, seq, 3 * inner)
        first.append(lax.psum_scatter(parts, "dp", scatter_dimension=0, tiled=False))
    cot_half = to_columns(cot, parity, dec, first[:1])
    cot_cols = halves(cot_half, mp_shift(cot_half, 1, dec), parity)
    cot_cols = [rows_of(cot_cols[:, b]) for b in range(mb)]
    cot_terms = jnp.concatenate([mm(c, w[3]).astype(BF16) for c in cot_cols], axis=1)
    dec_gctx = to_owner(cot_terms.reshape(n, seq, mb * inner), dec)
    w_relay = jnp.where(is_dec, w[2], mp_shift(w[1], 0, dec, flip=True))
    ctx_all, enc_out, kv_terms, kv_parts, keys = [], [], [], [], []
    for b in range(mb):
        qkv = [[(first[b], i * inner)] for i in range(3)]
        after = [*kv_terms[-1:], *dec_gctx[1:]] if b else []
        ctx = attend(info(section == 0, b), qkv, seq, inner, after)
        ctx = rows_of(gather(ctx, enc))
        ctx_all.append(gate(ctx, keys[-1]) if keys else ctx)
        terms = mm(ctx_all[b], w[3], NT).reshape(n, seq, depth)
        out, total, _ = relay(terms, raw_half[b], enc, 0, both)
        enc_out.append(out)
        terms = mm(rows_of(enc_out[b]), w_relay).astype(BF16).reshape(n, seq, inner)
        kv_terms.append(terms)
        kv_parts.append(to_owner(terms, both))
        key = functools.reduce(jnp.add, [k.astype(F32) for k in kv_parts[b]]).astype(BF16)
        keys.append(mp_shift(key, 0, enc, flip=True))
    relay_all, grad_enc, dec_send, dec_gram, dec_grads, ctx_terms = [], [], [], [], [], []
    for b in range(mb):
        operands = [
            [(first[b], 0)],
            [(keys[b], 0)],
            [(part, 0) for part in kv_parts[b]],
            [(part, b * inner) for part in dec_gctx],
        ]
        after = (total,) if b == 0 else ()
        gk, gv, send, gram = attend_back(
            info(section == 1, b), operands, seq, inner, True, (), after
        )
        dec_grads.append(jnp.where(is_dec, gv, mp_shift(gk, 0, dec, flip=True)))
        dec_send.append(send)
        dec_gram.append(gram)
    slots = []
    for b in range(mb):
        rows = gate(dec_grads[b], *kv_parts[-1][1:]) if b == 0 else dec_grads[b]
        slots.append(exchange(rows, both))
    for b in range(mb):
        rows = rows_of(in_order(slots[b]))
        relay_all.append(gate(rows, dec_grads[-1]) if b == 0 else rows)
        terms = mm(relay_all[b], w_relay, NT).reshape(n, seq, depth)
        after = slots[-1][1:] if b < mb - 1 else ()
        grad, _, got = relay(terms, None, both, 1, enc, after)
        grad_enc.append(grad)
        terms = mm(rows_of(grad_enc[b]), w[3]).astype(BF16)
        ctx_terms.append(terms.reshape(n, seq, inner))
    send_all, enc_gram = [], []
    for b in range(mb):
        gctx = to_owner(ctx_terms[b], enc)
        operands = [[(first[b], i * inner)] for i in range(3)] + [[(part, 0) for part in gctx]]
        after = got if b < mb - 1 else ()
        _, _, send, gram = attend_back(
            info(section == 0, b), operands, seq, inner, False, (dec_send[b],), after
        )
        enc_gram.append(gram)
        send_all.append(lax.all_gather(send, "dp", axis=0, tiled=True))
    normed = (own32 * inv[..., None] * gain).astype(BF16)
    gram_x = jnp.einsum("btd,bud->btu", normed, normed, preferred_element_type=F32)
    gram_cot = jnp.einsum("btd,bud->btu", cot, cot, preferred_element_type=F32)
    sq = []
    for b in range(mb):
        dg, eg = dec_gram[b], enc_gram[b]
        own = jnp.where(
            is_dec,
            jnp.sum(gram_x[b] * dg[0] + gram_cot[b] * dg[1]),
            jnp.sum(gram_x[b] * (eg[0] + eg[1])),
        )
        terms = jnp.where(is_dec, 0.0, gram_terms(grad_enc[b], ctx_all[b]))
        terms = terms + gram_terms(enc_out[b], relay_all[b])
        sq.append(terms + jnp.where(jnp.arange(n) == me, own, 0.0))
    sq = jnp.stack(sq)
    for axis, shift in (("mp", mp_shift), ("dp", dp_shift)):
        step = 1
        while step < lax.axis_size(axis):
            sq = sq + shift(sq, step, both)
            step *= 2
    sq = sq + mp_shift(sq, 0, both, flip=True)
    bound = jnp.sqrt(jnp.float32(8.0 * D * HEADS * HEAD))
    clip_all = bound / (jnp.sqrt(sq) + 0.01 * bound)
    clip = lax.dynamic_slice_in_dim(clip_all, me, 1, 1)[:, 0]
    flag = section.astype(jnp.int32)[None]
    out = dp_noise[0]
    for b in range(mb):
        xa = jnp.where(is_dec, cot_cols[b], x[b])
        xb = rows_of(jnp.where(is_dec, enc_out[b], grad_enc[b]))
        kept = jnp.where(is_dec, relay_all[b], ctx_all[b])
        out = wgrad(
            clip_all[b], flag, x[b], xa, xb, send_all[b], kept, out, seq, mb * n, b == 0
        )
    return (out[None], clip)


def solution(mesh):
    placed = (
        P("section", "dp", None, None),
        P("section", None),
        P("section", "dp", None, "mp"),
        P("dp", None, None),
        P(None, "dp"),
        P("section", "dp", None, "mp"),
    )
    return jax.shard_map(
        per_device,
        mesh=mesh,
        in_specs=placed,
        out_specs=(P("section", "dp", None, "mp"), P("dp")),
        check_vma=False,
    )
```

```python
import functools

import jax
import jax.numpy as jnp
from jax import lax
from jax.experimental import pallas as pl
from jax.experimental.pallas import tpu as pltpu
from jax.sharding import PartitionSpec as P

D = 4096
HEADS = 64
HEAD = 64
PAIR = 2 * HEAD
F32 = jnp.float32
BF16 = jnp.bfloat16
NN = (((1,), (0,)), ((), ()))
NT = (((1,), (1,)), ((), ()))
TN = (((0,), (0,)), ((), ()))


def mm(left, right, dims=NN):
    return lax.dot_general(left, right, dims, preferred_element_type=F32)


def dp_shift(x, distance, sections):
    n = lax.axis_size("dp")
    pairs = [(s * n + i, s * n + (i ^ distance)) for s in sections for i in range(n)]
    return lax.ppermute(x, ("section", "dp"), pairs)


def mp_shift(x, distance, sections, flip=False):
    n = lax.axis_size("mp")
    pairs = [
        (s * n + i, (1 - s if flip else s) * n + (i ^ distance)) for s in sections for i in range(n)
    ]
    return lax.ppermute(x, ("section", "mp"), pairs)


def pick(parts, index):
    return lax.dynamic_index_in_dim(parts, index, 0, keepdims=False)


def to_owner(parts, sections):
    n = lax.axis_size("dp")
    me = lax.axis_index("dp")
    got = [dp_shift(pick(parts, me ^ s), s, sections) for s in range(n - 1, 0, -1)]
    return [pick(parts, me)] + got


def in_order(slots):
    me = lax.axis_index("dp")
    stacked = jnp.stack(slots)
    return jnp.stack([pick(stacked, me ^ i) for i in range(len(slots))])


def exchange(rows, sections):
    n = lax.axis_size("dp")
    got = {s: dp_shift(rows, s, sections) for s in range(n - 1, 0, -1)}
    return [rows] + [got[s] for s in range(1, n)]


def gather(rows, sections):
    return in_order(exchange(rows, sections))


def halves(mine, other, parity):
    return jnp.where(
        parity == 0,
        jnp.concatenate([mine, other], axis=-2),
        jnp.concatenate([other, mine], axis=-2),
    )


def gate(x, *after):
    anywhere = pl.BlockSpec(memory_space=pl.ANY)

    def kernel(*refs):
        pass

    return pl.pallas_call(
        kernel,
        out_shape=jax.ShapeDtypeStruct(x.shape, x.dtype),
        in_specs=[anywhere] * (1 + len(after)),
        out_specs=anywhere,
        input_output_aliases={0: 0},
        name="gate",
    )(x, *after)


def to_columns(rows, parity, sections, after=()):
    n = lax.axis_size("dp")
    me = lax.axis_index("dp")
    half, width = rows.shape[1] // 2, rows.shape[2] // n
    rows = lax.dynamic_slice_in_dim(rows, parity * half, half, 1)
    if after:
        rows = gate(rows, *after)
    mine = [lax.dynamic_slice_in_dim(rows, (me ^ s) * width, width, 2) for s in range(n)]
    got = {s: dp_shift(mine[s], s, sections) for s in range(n - 1, 0, -1)}
    return in_order([mine[0]] + [got[s] for s in range(1, n)])


def relay(terms, residual, sources, giver, targets, after=()):
    groups = lax.axis_size("mp") // 2
    index = lax.axis_index("mp")
    parity = index % 2
    half = terms.shape[1] // 2
    low = terms.astype(BF16)
    keep = lax.dynamic_slice_in_dim(low, parity * half, half, 1)
    give = lax.dynamic_slice_in_dim(low, (1 - parity) * half, half, 1)
    total = keep.astype(F32) + mp_shift(give, 1, sources).astype(F32)
    if residual is not None:
        total = total + jnp.where(index < 2, residual.astype(F32), 0.0)
    total = total.astype(BF16)
    got = [mp_shift(total, 2 * g, (giver,), flip=True) for g in range(groups - 1, -1, -1)]
    got += [mp_shift(total, 2 * g, (0,)) for g in range(1, groups)]
    if after:
        got[-1] = gate(got[-1], *after)
    own = jnp.where(lax.axis_index("section") == 0, total.astype(F32), 0.0)
    mine = functools.reduce(jnp.add, [g.astype(F32) for g in got], own).astype(BF16)
    other = mp_shift(mine, 1, targets)
    return halves(mine, other, parity), total, got[-1]


def add_up(sources, start):
    terms = [ref[:, offset + start : offset + start + PAIR] for ref, offset in sources]
    if len(terms) == 1:
        return terms[0]
    return functools.reduce(jnp.add, [t.astype(F32) for t in terms]).astype(BF16)


def pair_masks(seq):
    lane = lax.broadcasted_iota(jnp.int32, (seq, PAIR), 1)
    return lane < HEAD


def stack_heads(x, first):
    zero = jnp.zeros_like(x)
    return jnp.concatenate([jnp.where(first, x, zero), jnp.where(first, zero, x)], axis=0)


def softmax_pair(scores, valid):
    seq = scores.shape[0]
    out = []
    for h in range(2):
        s = jnp.where(valid, scores[:, h * seq : (h + 1) * seq] * HEAD**-0.5, -jnp.inf)
        e = jnp.exp(s - jnp.max(s, axis=1, keepdims=True))
        out.append(e / jnp.sum(e, axis=1, keepdims=True))
    return jnp.concatenate(out, axis=1)


def plan_size(plan):
    return 1 + max(i for sources in plan for i, _ in sources)


def bind(plan, refs):
    return [[(refs[i], offset) for i, offset in sources] for sources in plan]


def fwd_kernel(plan, count, info, *refs):
    qs, ks, vs = bind(plan, refs)
    ctx_ref = refs[count]
    seq, width = ctx_ref.shape

    @pl.when(info[0] == 1)
    def run():
        first = pair_masks(seq)
        valid = lax.broadcasted_iota(jnp.int32, (seq, seq), 1) < info[1]
        for c in range(0, width, PAIR):
            q, k, v = add_up(qs, c), add_up(ks, c), add_up(vs, c)
            probs = softmax_pair(mm(q, stack_heads(k, first), NT), valid)
            ctx = mm(probs.astype(BF16), stack_heads(v, first))
            ctx_ref[:, c : c + PAIR] = ctx.astype(BF16)


def full_kernel(plan, count, decoder, info, *refs):
    qs, ks, vs, gs = bind(plan, refs)
    gk_ref, gv_ref, send_ref, gram_ref = refs[count:]
    seq, width = gk_ref.shape

    if not decoder:
        @pl.when(info[0] == 0)
        def hand_on():
            send_ref[...] = refs[plan_size(plan)][...]

    @pl.when(info[0] == 1)
    def run():
        first = pair_masks(seq)
        valid = lax.broadcasted_iota(jnp.int32, (seq, seq), 1) < info[1]
        grams = [jnp.zeros((seq, seq), F32) for _ in range(2)]
        for c in range(0, width, PAIR):
            q, k, v, g = add_up(qs, c), add_up(ks, c), add_up(vs, c), add_up(gs, c)
            k2, v2 = stack_heads(k, first), stack_heads(v, first)
            probs = softmax_pair(mm(q, k2, NT), valid)
            low = probs.astype(BF16)
            ctx = mm(low, v2).astype(BF16)
            gp = mm(g, v2, NT)
            ds = []
            for h in range(2):
                part = slice(h * seq, (h + 1) * seq)
                p, gph = probs[:, part], gp[:, part]
                inner = jnp.sum(gph * p, axis=1, keepdims=True)
                ds.append((p * (gph - inner) * HEAD**-0.5).astype(BF16))
            ds = jnp.concatenate(ds, axis=1)
            gq = mm(ds, k2).astype(BF16)
            gk = mm(ds, q, TN)
            gk = jnp.where(first, gk[:seq], gk[seq:]).astype(BF16)
            gv = mm(low, g, TN)
            gv = jnp.where(first, gv[:seq], gv[seq:]).astype(BF16)
            gk_ref[:, c : c + PAIR] = gk
            gv_ref[:, c : c + PAIR] = gv
            send_ref[:, c : c + PAIR] = gq
            send_ref[:, width + c : width + c + PAIR] = ctx if decoder else gk
            send_ref[:, 2 * width + c : 2 * width + c + PAIR] = gk if decoder else gv
            grams[0] += mm(gq, gq, NT)
            if decoder:
                grams[1] += mm(ctx, ctx, NT)
            else:
                grams[1] += mm(gk, gk, NT) + mm(gv, gv, NT)
        for i in range(2):
            gram_ref[i] = grams[i]


def call_attention(kernel, info, operands, outs, flops, name, extra=(), after=()):
    arrays, plan = [], []
    for sources in operands:
        plan.append([])
        for array, offset in sources:
            known = [i for i, a in enumerate(arrays) if a is array]
            if not known:
                arrays.append(array)
            plan[-1].append((known[0] if known else len(arrays) - 1, offset))
    arrays.extend(extra)
    vmem = pl.BlockSpec(memory_space=pltpu.VMEM)
    return pl.pallas_call(
        functools.partial(kernel, plan, len(arrays) + len(after)),
        out_shape=outs,
        in_specs=[pl.BlockSpec(memory_space=pltpu.SMEM)]
        + [vmem] * len(arrays)
        + [pl.BlockSpec(memory_space=pl.ANY)] * len(after),
        out_specs=(vmem,) * len(outs),
        compiler_params=pltpu.CompilerParams(vmem_limit_bytes=32 << 20),
        cost_estimate=pl.CostEstimate(
            flops=flops, bytes_accessed=sum(2 * a.size for a in arrays), transcendentals=0
        ),
        name=name,
    )(info, *arrays, *after)


def attend(info, operands, seq, width, after):
    rows = jax.ShapeDtypeStruct((seq, width), BF16)
    flops = 8 * seq * seq * width
    return call_attention(fwd_kernel, info, operands, (rows,), flops, "attend", (), after)[0]


def attend_back(info, operands, seq, width, decoder, extra=(), after=()):
    outs = (
        jax.ShapeDtypeStruct((seq, width), BF16),
        jax.ShapeDtypeStruct((seq, width), BF16),
        jax.ShapeDtypeStruct((seq, 3 * width), BF16),
        jax.ShapeDtypeStruct((2, seq, seq), F32),
    )

    def kernel(plan, count, *refs):
        full_kernel(plan, count, decoder, *refs)

    flops = 40 * seq * seq * width
    return call_attention(kernel, info, operands, outs, flops, "attend_back", extra, after)


def wgrad_kernel(count, chunk, scale, start, clip, info, x1, xa, xb, send, kept, base, out):
    width = out.shape[2]
    is_dec = info[0] == 1

    def clipped(ref):
        parts = [
            (ref[i * chunk : (i + 1) * chunk].astype(F32) * clip[i]).astype(BF16)
            for i in range(count)
        ]
        return jnp.concatenate(parts, axis=0)

    def put(slot, left, right, first):
        total = mm(left, right[:, first : first + width], TN)
        if start:
            out[:, slot, :] = (total + base[:, slot, :]) * scale
        else:
            out[:, slot, :] = total * scale + base[:, slot, :]

    l1, la, lb = clipped(x1), clipped(xa), clipped(xb)
    put(0, l1, send, 0)

    @pl.when(is_dec)
    def decoder():
        put(1, lb, send, 2 * width)
        put(2, lb, kept, 0)
        put(3, la, send, width)

    @pl.when(jnp.logical_not(is_dec))
    def encoder():
        put(1, la, send, width)
        put(2, l1, send, 2 * width)
        put(3, lb, kept, 0)


def wgrad(clip, info, x1, xa, xb, send, kept, base, chunk, examples, start):
    tokens, depth = x1.shape
    width = base.shape[2]
    block = 256
    smem = pl.BlockSpec(memory_space=pltpu.SMEM)
    left = pl.BlockSpec((tokens, block), lambda i: (0, i))
    wide = pl.BlockSpec((block, 4, width), lambda i: (i, 0, 0))
    once = [
        pl.BlockSpec(y.shape, lambda i: (0, 0), pipeline_mode=pl.Buffered(1)) for y in (send, kept)
    ]
    return pl.pallas_call(
        functools.partial(wgrad_kernel, tokens // chunk, chunk, 1.0 / examples, start),
        grid=(depth // block,),
        out_shape=jax.ShapeDtypeStruct(base.shape, F32),
        in_specs=[smem, smem, left, left, left] + once + [wide],
        out_specs=wide,
        compiler_params=pltpu.CompilerParams(vmem_limit_bytes=56 << 20),
        cost_estimate=pl.CostEstimate(
            flops=8 * tokens * depth * width,
            bytes_accessed=depth * 4 * width * 8 + tokens * width * 8,
            transcendentals=0,
        ),
        name="weight_gradient",
    )(clip, info, x1, xa, xb, send, kept, base)


def per_device(inputs, norm_gains, weights, cotangent, lengths, dp_noise):
    section = lax.axis_index("section")
    is_dec = section == 1
    me = lax.axis_index("dp")
    parity = lax.axis_index("mp") % 2
    n = lax.axis_size("dp")
    mb = inputs.shape[1]
    seq = inputs.shape[2]
    depth = weights.shape[1]
    inner = weights.shape[3]
    both, enc, dec = (0, 1), (0,), (1,)
    w = lax.optimization_barrier(jnp.transpose(weights[0], (1, 0, 2)))
    gain = norm_gains[0].astype(F32)
    gain_cols = lax.dynamic_slice_in_dim(gain, me * depth, depth)

    def rows_of(x):
        return x.reshape(n * seq, x.shape[-1])

    def grams(x):
        return jnp.einsum("itd,iud->itu", x, x, preferred_element_type=F32)

    def gram_terms(left, right):
        return jnp.sum(grams(left) * grams(right.reshape(n, seq, inner)), axis=(1, 2))

    def info(flag, b):
        return jnp.stack([flag.astype(jnp.int32), lengths[0, b]])

    own32 = inputs[0].astype(F32)
    inv = lax.rsqrt(jnp.mean(own32 * own32, axis=-1) + 1e-06)
    inv_all = gather(inv, both)
    raw_half, x = [], []
    for b in range(mb):
        mine = to_columns(inputs[0, b : b + 1], parity, both, raw_half[-1:])[:, 0]
        raw = halves(mine, mp_shift(mine, 1, both), parity)
        raw_half.append(mine)
        x.append(rows_of((raw.astype(F32) * inv_all[:, b, :, None] * gain_cols).astype(BF16)))
    keep = (jnp.arange(seq)[None] < lengths[1][:, None]).astype(BF16)
    cot = cotangent * keep[:, :, None]
    cot_half = to_columns(cot, parity, dec)
    cot_cols = halves(cot_half, mp_shift(cot_half, 1, dec), parity)
    cot_cols = [rows_of(cot_cols[:, b]) for b in range(mb)]
    first = []
    for b in range(mb):
        if b < mb - 1:
            parts = [mm(x[b], w[s]) for s in range(3)]
        else:
            w_k, w_v = jnp.where(is_dec, w[3], w[1]), jnp.where(is_dec, w[3], w[2])
            parts = [
                mm(x[b], w[0]),
                mm(jnp.where(is_dec, cot_cols[0], x[b]), w_k),
                mm(jnp.where(is_dec, cot_cols[1], x[b]), w_v),
            ]
        parts = jnp.concatenate([p.astype(BF16) for p in parts], axis=1)
        first.append(
            lax.psum_scatter(
                parts.reshape(n, seq, 3 * inner), "dp", scatter_dimension=0, tiled=False
            )
        )
    w_relay = jnp.where(is_dec, w[2], mp_shift(w[1], 0, dec, flip=True))
    ctx_all, enc_out, kv_terms, kv_parts, keys = [], [], [], [], []
    for b in range(mb):
        qkv = [[(first[b], i * inner)] for i in range(3)]
        ctx = attend(info(section == 0, b), qkv, seq, inner, kv_terms[-1:])
        ctx = rows_of(gather(ctx, enc))
        ctx_all.append(gate(ctx, keys[-1]) if keys else ctx)
        terms = mm(ctx_all[b], w[3], NT).reshape(n, seq, depth)
        out, total, posted = relay(terms, raw_half[b], enc, 0, both)
        enc_out.append(out)
        terms = mm(rows_of(enc_out[b]), w_relay).astype(BF16).reshape(n, seq, inner)
        kv_terms.append(terms)
        kv_parts.append(to_owner(terms, both))
        key = functools.reduce(jnp.add, [k.astype(F32) for k in kv_parts[b]]).astype(BF16)
        keys.append(mp_shift(key, 0, enc, flip=True))
    relay_all, grad_enc, dec_send, dec_gram, ctx_terms = [], [], [], [], []
    for b in range(mb):
        operands = [
            [(first[b], 0)],
            [(keys[b], 0)],
            [(part, 0) for part in kv_parts[b]],
            [(first[mb - 1], (1 + b) * inner)],
        ]
        after = (total,) if b == 0 else ()
        gk, gv, send, gram = attend_back(
            info(section == 1, b), operands, seq, inner, True, (), after
        )
        rows = jnp.where(is_dec, gv, mp_shift(gk, 0, dec, flip=True))
        if b == 0:
            rows = gate(rows, posted)
        slots = exchange(rows, both)
        rows = rows_of(in_order(slots))
        relay_all.append(gate(rows, ctx_terms[-1]) if ctx_terms else rows)
        terms = mm(relay_all[b], w_relay, NT).reshape(n, seq, depth)
        after = kv_terms[b + 1 : b + 2]
        grad, total, _ = relay(terms, None, both, 1, enc, after)
        grad_enc.append(grad)
        terms = mm(rows_of(grad_enc[b]), w[3]).astype(BF16)
        ctx_terms.append(terms.reshape(n, seq, inner))
        dec_send.append(send)
        dec_gram.append(gram)
    send_all, enc_gram = [], []
    for b in range(mb):
        gctx = to_owner(ctx_terms[b], enc)
        operands = [[(first[b], i * inner)] for i in range(3)] + [[(part, 0) for part in gctx]]
        _, _, send, gram = attend_back(
            info(section == 0, b),
            operands,
            seq,
            inner,
            False,
            (dec_send[b],),
            slots[1:] if b < mb - 1 else (),
        )
        enc_gram.append(gram)
        send_all.append(lax.all_gather(send, "dp", axis=0, tiled=True))
    normed = (own32 * inv[..., None] * gain).astype(BF16)
    gram_x = jnp.einsum("btd,bud->btu", normed, normed, preferred_element_type=F32)
    gram_cot = jnp.einsum("btd,bud->btu", cot, cot, preferred_element_type=F32)
    sq = []
    for b in range(mb):
        dg, eg = dec_gram[b], enc_gram[b]
        own = jnp.where(
            is_dec,
            jnp.sum(gram_x[b] * dg[0] + gram_cot[b] * dg[1]),
            jnp.sum(gram_x[b] * (eg[0] + eg[1])),
        )
        terms = jnp.where(is_dec, 0.0, gram_terms(grad_enc[b], ctx_all[b]))
        terms = terms + gram_terms(enc_out[b], relay_all[b])
        sq.append(terms + jnp.where(jnp.arange(n) == me, own, 0.0))
    sq = jnp.stack(sq)
    for axis, shift in (("mp", mp_shift), ("dp", dp_shift)):
        step = 1
        while step < lax.axis_size(axis):
            sq = sq + shift(sq, step, both)
            step *= 2
    sq = sq + mp_shift(sq, 0, both, flip=True)
    bound = jnp.sqrt(jnp.float32(8.0 * D * HEADS * HEAD))
    clip_all = bound / (jnp.sqrt(sq) + 0.01 * bound)
    clip = lax.dynamic_slice_in_dim(clip_all, me, 1, 1)[:, 0]
    flag = section.astype(jnp.int32)[None]
    out = dp_noise[0]
    for b in range(mb):
        xa = jnp.where(is_dec, cot_cols[b], x[b])
        xb = rows_of(jnp.where(is_dec, enc_out[b], grad_enc[b]))
        kept = jnp.where(is_dec, relay_all[b], ctx_all[b])
        out = wgrad(
            clip_all[b], flag, x[b], xa, xb, send_all[b], kept, out, seq, mb * n, b == 0
        )
    return (out[None], clip)


def solution(mesh):
    placed = (
        P("section", "dp", None, None),
        P("section", None),
        P("section", "dp", None, "mp"),
        P("dp", None, None),
        P(None, "dp"),
        P("section", "dp", None, "mp"),
    )
    return jax.shard_map(
        per_device,
        mesh=mesh,
        in_specs=placed,
        out_specs=(P("section", "dp", None, "mp"), P("dp")),
        check_vma=False,
    )
```
